256 devices in a mesh: tensor: 16 (over y_hi, z), fsdp: 8 (over x, core), dp: 2 (over y_lo).
Axes of the slice: x: 4, y: 4 (y_hi: 2, y_lo: 2; y = y_hi * 2 + y_lo), z: 8, core: 2. Of those that a mesh axis runs over, the one named last changes fastest.
Arguments:
- inputs: bfloat16 [16, 320, 4096], P(('fsdp', 'dp'), None, 'tensor'), may hold values from -6 to 6
- norm_gain: float32 [4096], P('tensor'), may hold values from 0.1 to 1.9
- gate_weight: bfloat16 [4096, 14336], P('fsdp', 'tensor'), may hold values from -0.09375 to 0.09375
- up_weight: bfloat16 [4096, 14336], P('fsdp', 'tensor'), may hold values from -0.09375 to 0.09375
- hidden_grad: bfloat16 [16, 320, 14336], P(('fsdp', 'dp'), None, 'tensor'), may hold values from -0.75 to 0.75
Outputs:
- input_grad: bfloat16 [16, 320, 4096], P(('fsdp', 'dp'), None, 'tensor')
- gain_grad: float32 [4096], P('tensor')
- gate_grad: bfloat16 [4096, 14336], P(('fsdp', 'dp'), 'tensor')
- up_grad: bfloat16 [4096, 14336], P(('fsdp', 'dp'), 'tensor')
The draws below stay inside these ranges and needn't reach their ends.
All inputs are finite; a program needn't handle non-finite values.
Results may differ from the reference program's by a relative error of at most 0.03.
Values may be sent and summed in bfloat16 or wider, within the bound.
No kernel may reach another device: no remote copies, remote signals or barrier semaphores. Data moves between devices by JAX's collectives and lax.ppermute only.
A program may use at most 128 MiB of HBM per device.

```python
import jax
import jax.numpy as jnp
from jax import lax

D = 4096
FF = 14336
TOK_GRP = 320
GROUPS = 16
FFD = 896
N_TENSOR = 16


def raised(result, rng, source, target, parts, factor):
    owner, partner = [(jnp.arange(result.shape[dim]) // (result.shape[dim] // parts)).reshape([-1 if axis == dim else 1 for axis in range(result.ndim)]) for dim in (source, target)]
    chosen = jax.random.permutation(rng, parts)[partner]
    strong = (owner == chosen) | (owner == (partner + parts // 2) % parts)
    return jnp.where(strong, factor * result, result)


def block_scale(key, extent, split, least, largest):
    def one(dim, parts):
        steps = jax.random.uniform(jax.random.fold_in(jax.random.fold_in(key, 6), dim), (parts,), jnp.float32, least / len(split), largest / len(split))
        return jnp.repeat(jnp.exp(steps), extent[dim] // parts).reshape((-1,) + (1,) * (len(extent) - dim - 1))

    factor_of = one(*split[0])
    for cut in split[1:]:
        factor_of = factor_of * one(*cut)
    return factor_of


def centred(own_key, extent, deviation, most, cuts=(), held_as=jnp.bfloat16):
    drawn = jax.random.normal(own_key, extent, jnp.float32) * deviation
    if len(cuts) > 0:
        drawn = block_scale(own_key, extent, cuts, -0.22, 0.18) * drawn
    return jnp.clip(drawn, min=-most, max=most).astype(held_as)


def heavy_noise(key, extent, deviation, bound, shards, heavy, dtype=jnp.bfloat16):
    result = deviation * jax.random.normal(key, extent, jnp.float32)
    if shards:
        result = result * block_scale(key, extent, shards, -0.22, 0.18)
    return jnp.clip(raised(result, jax.random.fold_in(key, 3), *heavy), -bound, bound).astype(dtype)


def setup_inputs(seed: int = 0) -> dict:
    seeds = jax.random.split(jax.random.key(seed), 6)
    return {
        "inputs": heavy_noise(seeds[0], (GROUPS, TOK_GRP, D), 1.0, 6.0, ((0, 16), (2, 16)), (0, 2, 16, 2.0)),
        "norm_gain": jnp.clip(1.0 + 0.18 * jax.random.normal(seeds[1], (D,), jnp.float32), 0.1, 1.9),
        "gate_weight": centred(seeds[2], (D, FF), D ** -0.5, 0.09375, ((0, 8), (1, 16))),
        "up_weight": centred(seeds[3], (D, FF), D ** -0.5, 0.09375, ((0, 8), (1, 16))),
        "hidden_grad": centred(seeds[4], (GROUPS, TOK_GRP, FF), 0.05, 0.75, ((0, 16), (2, 16))),
    }


norm_epsilon = 1e-05

def reference(inputs, norm_gain, gate_weight, up_weight, hidden_grad):
    source = inputs.astype(jnp.float32).reshape(GROUPS * TOK_GRP, D)
    inverse_rms = lax.rsqrt(lax.optimization_barrier(jnp.mean(source * source, axis=-1, keepdims=True)) + norm_epsilon)
    normed = (source * inverse_rms * norm_gain).astype(jnp.bfloat16)
    gate_value = jnp.dot(normed, gate_weight, preferred_element_type=jnp.float32)
    up_value = jnp.dot(normed, up_weight, preferred_element_type=jnp.float32)
    upstream = hidden_grad.reshape(GROUPS * TOK_GRP, FF).astype(jnp.float32)
    sigmoid_gate = jax.nn.sigmoid(gate_value)
    up_slope = (upstream * gate_value * sigmoid_gate).astype(jnp.bfloat16)
    gate_slope = (upstream * up_value * sigmoid_gate * (1.0 + gate_value * (1.0 - sigmoid_gate))).astype(jnp.bfloat16)
    contract_units = (((1,), (1,)), ((), ()))

    def add_block(member, total):
        begin_unit = (member * FFD).astype(jnp.int32)
        slope_a = lax.dynamic_slice_in_dim(gate_slope, begin_unit, FFD, 1)
        slope_b = lax.dynamic_slice_in_dim(up_slope, begin_unit, FFD, 1)
        weight_a = lax.dynamic_slice_in_dim(gate_weight, begin_unit, FFD, 1)
        weight_b = lax.dynamic_slice_in_dim(up_weight, begin_unit, FFD, 1)
        block_sum = lax.dot_general(slope_a, weight_a, contract_units, preferred_element_type=jnp.float32)
        block_sum = block_sum + lax.dot_general(slope_b, weight_b, contract_units, preferred_element_type=jnp.float32)
        rounded = lax.optimization_barrier(block_sum.astype(jnp.bfloat16))
        return total + rounded.astype(jnp.float32)
    normed_grad = lax.fori_loop(0, N_TENSOR, add_block, jnp.zeros((GROUPS * TOK_GRP, D), jnp.float32))
    weighted = normed_grad * norm_gain
    correction = lax.optimization_barrier(jnp.mean(weighted * source, axis=-1, keepdims=True))
    input_grad = inverse_rms * weighted - source * inverse_rms * inverse_rms * inverse_rms * correction
    gain_grad = lax.optimization_barrier(jnp.sum(normed_grad * source * inverse_rms, axis=0))
    normed_groups = normed.reshape(GROUPS, TOK_GRP, D)
    gate_groups = gate_slope.reshape(GROUPS, TOK_GRP, FF)
    up_groups = up_slope.reshape(GROUPS, TOK_GRP, FF)
    contract_tokens = (((0,), (0,)), ((), ()))

    def add_group(member, totals):
        gate_total, up_total = totals
        index = jnp.asarray(member).astype(jnp.int32)
        group_normed = lax.dynamic_index_in_dim(normed_groups, index, 0, keepdims=False)
        group_gate = lax.dynamic_index_in_dim(gate_groups, index, 0, keepdims=False)
        group_up = lax.dynamic_index_in_dim(up_groups, index, 0, keepdims=False)
        gate_part = lax.dot_general(group_normed, group_gate, contract_tokens, preferred_element_type=jnp.float32)
        up_part = lax.dot_general(group_normed, group_up, contract_tokens, preferred_element_type=jnp.float32)
        gate_part = lax.optimization_barrier(gate_part.astype(jnp.bfloat16)).astype(jnp.float32)
        up_part = lax.optimization_barrier(up_part.astype(jnp.bfloat16)).astype(jnp.float32)
        return (gate_total + gate_part, up_total + up_part)
    empty = jnp.zeros((D, FF), jnp.float32)
    gate_total, up_total = lax.fori_loop(0, GROUPS, add_group, (empty, empty))
    return (input_grad.reshape(GROUPS, TOK_GRP, D).astype(jnp.bfloat16), gain_grad, gate_total.astype(jnp.bfloat16), up_total.astype(jnp.bfloat16))
```

```python
import functools

import jax
import jax.numpy as jnp
import numpy as np
from jax import lax
from jax.experimental import pallas as pl
from jax.experimental.pallas import tpu as pltpu
from jax.sharding import PartitionSpec as P

norm_epsilon = 1e-05
AXES = ("tensor", "fsdp", "dp")
NX, NY, NZ = 4, 4, 8
BF = jnp.bfloat16
F32 = jnp.float32
TOK = 320
BLK = 256
FEATS = 4096
UNITS = 896
EXTRA = 16
ROWS_A = 176
TOK_A = ROWS_A - EXTRA
ROWS_B = TOK - TOK_A
FULL = 384
HALF = 64


def _index(x, c, y, z):
    return (((y % NY) // 2) * NZ + z % NZ) * 16 + ((x % NX) * 2 + c % 2) * 2 + y % 2


def _pairs(dx=0, dc=0, dy=0, dz=0, dp=False):
    pairs = []
    for x in range(NX):
        for c in range(2):
            for y in range(NY):
                for z in range(NZ):
                    to = y ^ 1 if dp else y + dy
                    pairs.append((_index(x, c, y, z), _index(x + dx, c + dc, to, z + dz)))
    return pairs


def move(value, **step):
    return lax.ppermute(value, AXES, _pairs(**step))


def add(*terms):
    total = terms[0].astype(F32)
    for term in terms[1:]:
        total = total + term.astype(F32)
    return total


def forward_kernel(idx, own, par, w, grad, slopes, corr, inverse, acc, square):
    step = pl.program_id(0)

    @pl.when(step == 0)
    def _():
        acc[...] = jnp.zeros_like(acc)
        square[...] = jnp.zeros_like(square)

    weight = w[...]
    for m, ref in enumerate((own, par)):
        gain = ref[0, 0, 0:1, :].astype(F32) + ref[0, 0, 1:2, :].astype(F32)
        x = ref[0, 0, EXTRA:, :].astype(F32)
        sq = x * x
        rows = pl.ds(m * TOK, TOK)
        square[rows, :] += sq[:, :128] + sq[:, 128:]
        acc[rows, :] += jnp.dot((x * gain).astype(BF), weight, preferred_element_type=F32)

    @pl.when(step == pl.num_programs(0) - 1)
    def _():
        for m in range(2):
            rows = pl.ds(m * TOK, TOK)
            inv = lax.rsqrt(jnp.sum(square[rows, :], axis=-1, keepdims=True) / FEATS + norm_epsilon)

            def slope_pair(gate, up, upstream):
                s = 1.0 / (1.0 + jnp.exp(-gate))
                down = (upstream * up * s * (1.0 + gate * (1.0 - s))).astype(BF)
                lift = (upstream * gate * s).astype(BF)
                return down, lift

            total = jnp.zeros((TOK, 1), F32)
            for tile in range(FULL // 128):
                here, there = pl.ds(tile * 128, 128), pl.ds(FULL + 128 + tile * 128, 128)
                gate, up = acc[rows, here] * inv, acc[rows, there] * inv
                down, lift = slope_pair(gate, up, grad[m, :, here].astype(F32))
                slopes[m, :, here] = down
                slopes[m, :, there] = lift
                total += jnp.sum(
                    down.astype(F32) * gate + lift.astype(F32) * up, axis=-1, keepdims=True
                )
            mixed = acc[rows, pl.ds(FULL, 128)] * inv
            turned = pltpu.roll(mixed, HALF, 1)
            first = lax.broadcasted_iota(jnp.int32, (TOK, 128), 1) < HALF
            gate, up = jnp.where(first, mixed, turned), jnp.where(first, turned, mixed)
            down, lift = slope_pair(gate, up, grad[m, :, pl.ds(FULL, 128)].astype(F32))
            both = jnp.where(first, down.astype(F32), lift.astype(F32))
            slopes[m, :, pl.ds(FULL, 128)] = both.astype(BF)
            total += jnp.sum(both * mixed, axis=-1, keepdims=True)
            corr[m] = total / inv
            inverse[m] = inv


def input_kernel(idx, slopes, w, extra, out_a, out_b):
    m = pl.program_id(1)
    part = lax.dot_general(
        slopes[m], w[...], (((1,), (1,)), ((), ())), preferred_element_type=F32
    ).astype(BF)
    out_a[0, 0, :EXTRA, :] = extra[m]
    out_a[0, 0, EXTRA:, :] = part[:TOK_A]
    out_b[0, 0] = part[TOK_A:]


def weight_kernel(idx, own, par, inverse, slopes, out):
    total = None
    for m, ref in enumerate((own, par)):
        gain = ref[0, 0, 0:1, :].astype(F32) + ref[0, 0, 1:2, :].astype(F32)
        normed = (ref[0, 0, EXTRA:, :].astype(F32) * (inverse[m] * gain)).astype(BF)
        term = lax.dot_general(
            normed, slopes[m], (((0,), (0,)), ((), ())), preferred_element_type=F32
        )
        total = term if total is None else total + term
    out[0] = total.astype(BF)


LIMIT = 56 * 1024 * 1024


def _params(dims):
    return pltpu.CompilerParams(
        dimension_semantics=("arbitrary",) * dims, vmem_limit_bytes=LIMIT
    )


def _cost(flops, moved, exps=0):
    return pl.CostEstimate(flops=flops, bytes_accessed=moved, transcendentals=exps)


def forward(idx, stack, weights, grad):
    block = (1, 1, EXTRA + TOK, BLK)
    return pl.pallas_call(
        forward_kernel,
        grid_spec=pltpu.PrefetchScalarGridSpec(
            num_scalar_prefetch=1,
            grid=(16,),
            in_specs=[
                pl.BlockSpec(block, lambda k, i: (2 * (k // 8), k % 8, 0, 0)),
                pl.BlockSpec(block, lambda k, i: (i[16 + k // 8], k % 8, 0, 0)),
                pl.BlockSpec((BLK, UNITS), lambda k, i: (i[k], 0)),
                pl.BlockSpec((2, TOK, 512), lambda k, i: (0, 0, 0)),
            ],
            out_specs=[
                pl.BlockSpec((2, TOK, UNITS), lambda k, i: (0, 0, 0)),
                pl.BlockSpec((2, TOK, 1), lambda k, i: (0, 0, 0)),
                pl.BlockSpec((2, TOK, 1), lambda k, i: (0, 0, 0)),
            ],
            scratch_shapes=[
                pltpu.VMEM((2 * TOK, UNITS), F32),
                pltpu.VMEM((2 * TOK, 128), F32),
            ],
        ),
        out_shape=[
            jax.ShapeDtypeStruct((2, TOK, UNITS), BF),
            jax.ShapeDtypeStruct((2, TOK, 1), F32),
            jax.ShapeDtypeStruct((2, TOK, 1), F32),
        ],
        compiler_params=_params(1),
        cost_estimate=_cost(2 * 640 * FEATS * UNITS, 14 << 20, 640 * 512),
        name="forward_slopes",
    )(idx, stack, stack, weights, grad)


def input_parts(idx, slopes, weights, extra):
    return pl.pallas_call(
        input_kernel,
        grid_spec=pltpu.PrefetchScalarGridSpec(
            num_scalar_prefetch=1,
            grid=(16, 2),
            in_specs=[
                pl.BlockSpec((2, TOK, UNITS), lambda k, m, i: (0, 0, 0)),
                pl.BlockSpec((BLK, UNITS), lambda k, m, i: (i[k], 0)),
                pl.BlockSpec((2, EXTRA, BLK), lambda k, m, i: (0, 0, 0)),
            ],
            out_specs=[
                pl.BlockSpec((1, 1, ROWS_A, BLK), lambda k, m, i: (i[18 + 2 * m + k // 8], k % 8, 0, 0)),
                pl.BlockSpec((1, 1, ROWS_B, BLK), lambda k, m, i: (k % 8, i[18 + 2 * m + k // 8], 0, 0)),
            ],
        ),
        out_shape=[
            jax.ShapeDtypeStruct((NY, NZ, ROWS_A, BLK), BF),
            jax.ShapeDtypeStruct((NZ, NY, ROWS_B, BLK), BF),
        ],
        compiler_params=_params(2),
        cost_estimate=_cost(2 * 640 * FEATS * UNITS, 14 << 20),
        name="input_parts",
    )(idx, slopes, weights, extra)


def weight_parts(idx, stack, inverse, slopes):
    block = (1, 1, EXTRA + TOK, BLK)
    return pl.pallas_call(
        weight_kernel,
        grid_spec=pltpu.PrefetchScalarGridSpec(
            num_scalar_prefetch=1,
            grid=(8,),
            in_specs=[
                pl.BlockSpec(block, lambda s, i: (i[s], i[16 + s], 0, 0)),
                pl.BlockSpec(block, lambda s, i: (i[8 + s], i[16 + s], 0, 0)),
                pl.BlockSpec((2, TOK, 1), lambda s, i: (0, 0, 0)),
                pl.BlockSpec((2, TOK, UNITS), lambda s, i: (0, 0, 0)),
            ],
            out_specs=pl.BlockSpec((1, BLK, UNITS), lambda s, i: (s, 0, 0)),
        ),
        out_shape=jax.ShapeDtypeStruct((8, BLK, UNITS), BF),
        compiler_params=_params(1),
        cost_estimate=_cost(640 * FEATS * UNITS, 7 << 20),
        name="weight_parts",
    )(idx, stack, stack, inverse, slopes)


def gather_plane(shard, gain):
    high = gain.astype(BF)
    low = (gain - high.astype(F32)).astype(BF)
    head = jnp.concatenate([high[None], low[None], jnp.zeros((EXTRA - 2, BLK), BF)], axis=0)
    part_a = jnp.concatenate([head, shard[:TOK_A]], axis=0)
    part_b = shard[TOK_A:]
    b1, b3, b2 = move(part_b, dy=-1), move(part_b, dy=1), move(part_b, dy=2)
    column = jnp.stack([part_b, b1, b2, b3])
    rows = {0: column}
    for p in (1, 2, 3):
        rows[p] = move(rows[p - 1], dz=-1)
        rows[8 - p] = move(rows[(9 - p) % 8], dz=1)
    rows[4] = jnp.concatenate([move(rows[3][:2], dz=-1), move(rows[5][2:], dz=1)], axis=0)
    line = {p: move(part_a, dz=-p) for p in (4, 3, 5, 2, 6, 1, 7)}
    line[0] = part_a
    a0 = jnp.stack([line[p] for p in range(NZ)])
    a1, a3 = move(a0, dy=-1), move(a0, dy=1)
    a2 = jnp.concatenate([move(a1[:4], dy=-1), move(a3[4:], dy=1)], axis=0)
    whole_a = jnp.stack([a0, a1, a2, a3])
    whole_b = jnp.stack([rows[p] for p in range(NZ)], axis=1)
    return jnp.concatenate([whole_a, whole_b], axis=2)


def scatter_plane(part_a, part_b):
    half = NZ // 2
    far_up, far_down = move(part_a[2, :half], dy=1), move(part_a[2, half:], dy=-1)
    plain_up, plain_down = move(part_a[1, half:], dy=1), move(part_a[3, :half], dy=-1)
    sum_up = move(add(part_a[1, :half], far_up).astype(BF), dy=1)
    sum_down = move(add(part_a[3, half:], far_down).astype(BF), dy=-1)
    up, down = move(part_b[4, :2], dz=1), move(part_b[4, 2:], dz=-1)
    up = jnp.concatenate([add(part_b[3, :2], up).astype(BF), part_b[3, 2:]], axis=0)
    down = jnp.concatenate([part_b[5, :2], add(part_b[5, 2:], down).astype(BF)], axis=0)
    up, down = move(up, dz=1), move(down, dz=-1)
    for p in (2, 1):
        up = move(add(part_b[p], up).astype(BF), dz=1)
        down = move(add(part_b[8 - p], down).astype(BF), dz=-1)
    low = add(part_a[0, :half], sum_up, plain_down)
    high = add(part_a[0, half:], plain_up, sum_down)
    line = jnp.concatenate([low, high], axis=0)
    sent = line.astype(BF)
    sum_a = add(line[0], *[move(sent[p], dz=p) for p in (4, 3, 5, 2, 6, 1, 7)])
    column = add(part_b[0], up, down)
    sent = column.astype(BF)
    sum_b = add(column[0], move(sent[1], dy=1), move(sent[3], dy=3), move(sent[2], dy=2))
    return sum_a, sum_b


def pick(first, second, d):
    return jnp.where(d == 0, first, second)


def mine(left, right, d):
    rest = FULL + 2 * HALF
    return jnp.concatenate(
        [
            pick(left[:, :FULL], left[:, rest:], d),
            pick(left[:, FULL : FULL + HALF], left[:, FULL + HALF : rest], d),
            pick(right[:, FULL : FULL + HALF], right[:, FULL + HALF : rest], d),
            pick(right[:, :FULL], right[:, rest:], d),
        ],
        axis=1,
    )


def tables():
    tensor, fsdp, d = (lax.axis_index(axis).astype(jnp.int32) for axis in AXES)
    y_hi, z = tensor // NZ, tensor % NZ
    x, c = fsdp // 2, fsdp % 2
    k = jnp.arange(16, dtype=jnp.int32)
    block = ((y_hi + k // 8) % 2) * NZ + (z + k % 8) % NZ
    partner = jnp.stack([1 + 2 * d, 3 - 2 * d])
    first = jnp.concatenate([block, partner, jnp.array([0, 2], jnp.int32), partner])

    def of_core(core):
        s = jnp.arange(8, dtype=jnp.int32)
        g = (((x + s // 2) % NX) * 2 + core) * 2 + s % 2
        h, p = (g // NZ - y_hi) % 2, (g % NZ - z) % NZ
        return jnp.concatenate([2 * h, 1 + 2 * ((d + h) % 2), p])

    return first, of_core(1 - c), of_core(c), d


def body(inputs, norm_gain, gate_weight, up_weight, hidden_grad):
    first, other_core, this_core, d = tables()
    weights = lax.all_gather(mine(gate_weight, up_weight, d), "fsdp", axis=0, tiled=True)

    grad = hidden_grad[0]
    keep = mine(grad, grad, d)[:, : FULL + 128]
    give = mine(grad, grad, 1 - d)[:, : FULL + 128]
    grads = jnp.stack([keep, move(give, dp=True)])

    local_x = inputs[0]
    stack = gather_plane(local_x, norm_gain)
    slopes, corr, inverse = forward(first, stack, weights, grads)

    rows = jnp.pad(corr[:, :, 0] / FEATS, ((0, 0), (0, 512 - TOK))).reshape(2, 2, BLK)
    extra = jnp.pad(rows, ((0, 0), (0, EXTRA - 2), (0, 0))).astype(BF)
    part_a, part_b = input_parts(first, slopes, weights, extra)

    theirs = weight_parts(other_core, stack, inverse, slopes)
    got = move(theirs, dc=1)
    ours = weight_parts(this_core, stack, inverse, slopes)
    blocks = add(ours, got).astype(BF)

    sum_a, sum_b = scatter_plane(part_a, part_b)

    far_up, far_down = move(blocks[4], dx=1), move(blocks[5], dx=-1)
    plain_up, plain_down = move(blocks[3], dx=1), move(blocks[6], dx=-1)
    sum_up = move(add(blocks[2], far_up).astype(BF), dx=1)
    sum_down = move(add(blocks[7], far_down).astype(BF), dx=-1)
    rows_0 = add(blocks[0], sum_up, plain_down)
    rows_1 = add(blocks[1], plain_up, sum_down)
    keep = pick(rows_0, rows_1, d).astype(BF)
    got = move(pick(rows_1, rows_0, d).astype(BF), dp=True)

    def whole(start, shared):
        left, right = pick(keep, got, d), pick(got, keep, d)
        return jnp.concatenate(
            [
                left[:, start : start + FULL],
                left[:, shared : shared + HALF],
                right[:, shared : shared + HALF],
                right[:, start : start + FULL],
            ],
            axis=1,
        )

    gate_grad = whole(0, FULL)
    up_grad = whole(FULL + 128, FULL + HALF)

    normed_grad = jnp.concatenate([sum_a[EXTRA:], sum_b], axis=0)
    correction = sum_a[:2].reshape(512)[:TOK][:, None]
    inv = inverse[0]
    x = local_x.astype(F32)
    input_grad = inv * (normed_grad * norm_gain) - x * inv * inv * inv * correction
    gain_part = jnp.sum(normed_grad * x * inv, axis=0).reshape(2, 128)
    gain_part = gain_part + move(gain_part, dc=1)
    gain_part = (
        gain_part + move(gain_part, dx=1) + move(gain_part, dx=-1) + move(gain_part, dx=2)
    )
    gain_grad = (gain_part + move(gain_part, dp=True)).reshape(BLK)
    return input_grad.astype(BF)[None], gain_grad, gate_grad, up_grad


def solution(mesh):
    placed = (
        P(("fsdp", "dp"), None, "tensor"),
        P("tensor"),
        P("fsdp", "tensor"),
        P("fsdp", "tensor"),
        P(("fsdp", "dp"), None, "tensor"),
    )
    return jax.shard_map(
        body,
        mesh=mesh,
        in_specs=placed,
        out_specs=(
            P(("fsdp", "dp"), None, "tensor"),
            P("tensor"),
            P(("fsdp", "dp"), "tensor"),
            P(("fsdp", "dp"), "tensor"),
        ),
        check_vma=False,
    )
```

```python
import jax
import jax.numpy as jnp
from jax import lax
from jax.experimental import pallas as pl
from jax.experimental.pallas import tpu as pltpu
from jax.sharding import PartitionSpec as P

norm_epsilon = 1e-05
AXES = ("tensor", "fsdp", "dp")
NX, NY, NZ = 4, 4, 8
BF = jnp.bfloat16
F32 = jnp.float32
TOK = 320
BLK = 256
FEATS = 4096
UNITS = 896
EXTRA = 16
ROWS_A = 176
TOK_A = ROWS_A - EXTRA
ROWS_B = TOK - TOK_A
FULL = 384
HALF = 64


def _index(x, c, y, z):
    return (((y % NY) // 2) * NZ + z % NZ) * 16 + ((x % NX) * 2 + c % 2) * 2 + y % 2


def _pairs(dx=0, dc=0, dy=0, dz=0, flip=0, turn=False):
    pairs = []
    for x in range(NX):
        for c in range(2):
            way = -1 if turn and c else 1
            for y in range(NY):
                for z in range(NZ):
                    to = (y ^ flip) + way * dy
                    there = _index(x + way * dx, c + dc, to, z + way * dz)
                    pairs.append((_index(x, c, y, z), there))
    return pairs


def move(value, **step):
    return lax.ppermute(value, AXES, _pairs(**step))


def add(*terms):
    total = terms[0].astype(F32)
    for term in terms[1:]:
        total = total + term.astype(F32)
    return total


CHUNK = 64


def forward_kernel(idx, *refs):
    a0, a1, a2_low, a2_high, a3 = refs[:5]
    rows_b = refs[5:14]
    w, grad, scaled, slopes, ready, corr, inverse, acc, square, held, sems = refs[14:]

    def fetch(k):
        there = pl.ds(pl.multiple_of(idx[k] * BLK, BLK), BLK)
        return pltpu.make_async_copy(w.at[there], held.at[pl.ds(k * BLK, BLK)], sems.at[k])

    for k in range(16):
        fetch(k).start()
    for m in range(2):
        square[pl.ds(m * TOK, TOK), :] = jnp.zeros((TOK, 128), F32)
    for group in range(4):
        h, quad = group // 2, group % 2
        for m in range(2):
            if (h, m) == (1, 0):
                block_a, start = (a2_low, a2_high)[quad], 0
            else:
                block_a, start = {(0, 0): a0, (0, 1): a1, (1, 1): a3}[h, m], 4 * quad
            j = 2 * h + m
            sums_a, sums_b = [], []
            for q in range(4):
                p = 4 * quad + q
                head = block_a[start + q, 0:2, :].astype(F32)
                gain = head[0:1] + head[1:2]
                lanes = pl.ds((4 * group + q) * BLK, BLK)
                x = block_a[start + q, EXTRA:, :].astype(F32)
                scaled[pl.ds(m * TOK, TOK_A), lanes] = (x * gain).astype(BF)
                sq = x * x
                sums_a.append(sq[:, :128] + sq[:, 128:])
                block_b = rows_b[p][j] if p < 4 else rows_b[p + 1][j] if p > 4 else rows_b[4 + j // 2][j % 2]
                x = block_b.astype(F32)
                scaled[pl.ds(m * TOK + TOK_A, ROWS_B), lanes] = (x * gain).astype(BF)
                sq = x * x
                sums_b.append(sq[:, :128] + sq[:, 128:])
            square[pl.ds(m * TOK, TOK_A), :] += sum(sums_a[1:], sums_a[0])
            square[pl.ds(m * TOK + TOK_A, ROWS_B), :] += sum(sums_b[1:], sums_b[0])
        for q in range(4):
            fetch(4 * group + q).wait()
        lanes = pl.ds(4 * group * BLK, 4 * BLK)
        product = jnp.dot(scaled[:, lanes], held[lanes, :], preferred_element_type=F32)
        acc[...] = product if group == 0 else acc[...] + product

    first = lax.broadcasted_iota(jnp.int32, (CHUNK, 128), 1) < HALF

    def slope_pair(gate, up, upstream):
        s = 1.0 / (1.0 + jnp.exp(-gate))
        return upstream * up * s * (1.0 + gate * (1.0 - s)), upstream * gate * s

    for chunk in range(2 * TOK // CHUNK):
        rows = pl.ds(chunk * CHUNK, CHUNK)
        mean = jnp.sum(square[rows, :], axis=-1, keepdims=True) / FEATS
        inv = lax.rsqrt(mean + norm_epsilon)
        total = jnp.zeros((CHUNK, 128), F32)
        for tile in range(FULL // 128):
            here, there = pl.ds(tile * 128, 128), pl.ds(FULL + 128 + tile * 128, 128)
            gate, up = acc[rows, here] * inv, acc[rows, there] * inv
            down, lift = slope_pair(gate, up, grad[rows, here].astype(F32))
            slopes[rows, here] = down.astype(BF)
            slopes[rows, there] = lift.astype(BF)
            ready[rows, here] = (down * inv).astype(BF)
            ready[rows, there] = (lift * inv).astype(BF)
            total += down * gate + lift * up
        here = pl.ds(FULL, 128)
        mixed = acc[rows, here] * inv
        turned = pltpu.roll(mixed, HALF, 1)
        gate, up = jnp.where(first, mixed, turned), jnp.where(first, turned, mixed)
        down, lift = slope_pair(gate, up, grad[rows, here].astype(F32))
        both = jnp.where(first, down, lift)
        slopes[rows, here] = both.astype(BF)
        ready[rows, here] = (both * inv).astype(BF)
        total += both * mixed
        corr[rows, :] = jnp.sum(total, axis=-1, keepdims=True) / inv
        inverse[rows, :] = inv


def input_kernel(idx, slopes, w0, w1, w2, w3, extra, own_a, par_a, out_b):
    for q, w in enumerate((w0, w1, w2, w3)):
        part = lax.dot_general(
            slopes[...], w[...], (((1,), (1,)), ((), ())), preferred_element_type=F32
        ).astype(BF)
        own_a[0, q, :EXTRA, :] = extra[0]
        own_a[0, q, EXTRA:, :] = part[:TOK_A]
        out_b[q, 0] = part[TOK_A:TOK]
        par_a[0, q, :EXTRA, :] = extra[1]
        par_a[0, q, EXTRA:, :] = part[TOK : TOK + TOK_A]
        out_b[q, 1] = part[TOK + TOK_A :]


def weight_kernel(idx, x0, x1, x2, x3, ready, before, out):
    for q, x in enumerate((x0, x1, x2, x3)):
        out[q] = lax.dot_general(
            x[...], ready[...], (((0,), (0,)), ((), ())), preferred_element_type=F32
        ).astype(BF)


LIMIT = 56 * 1024 * 1024


def _params(dims):
    return pltpu.CompilerParams(
        dimension_semantics=("arbitrary",) * dims, vmem_limit_bytes=LIMIT
    )


def _cost(flops, moved, exps=0):
    return pl.CostEstimate(flops=flops, bytes_accessed=moved, transcendentals=exps)


def _still(*shape):
    return pl.BlockSpec(shape, lambda *_: (0,) * len(shape))


def forward(idx, pieces, weights, grad):
    smem = pl.BlockSpec(memory_space=pltpu.SMEM)
    vmem = pl.BlockSpec(memory_space=pltpu.VMEM)
    return pl.pallas_call(
        forward_kernel,
        in_specs=[smem, *[vmem] * 14, pl.BlockSpec(memory_space=pl.ANY), vmem],
        out_specs=[vmem] * 5,
        scratch_shapes=[
            pltpu.VMEM((2 * TOK, UNITS), F32),
            pltpu.VMEM((2 * TOK, 128), F32),
            pltpu.VMEM((FEATS, UNITS), BF),
            pltpu.SemaphoreType.DMA((16,)),
        ],
        out_shape=[
            jax.ShapeDtypeStruct((2 * TOK, FEATS), BF),
            jax.ShapeDtypeStruct((2 * TOK, UNITS), BF),
            jax.ShapeDtypeStruct((2 * TOK, UNITS), BF),
            jax.ShapeDtypeStruct((2 * TOK, 1), F32),
            jax.ShapeDtypeStruct((2 * TOK, 1), F32),
        ],
        compiler_params=pltpu.CompilerParams(vmem_limit_bytes=LIMIT),
        cost_estimate=_cost(2 * 640 * FEATS * UNITS, 14 << 20, 640 * 512),
        name="forward_slopes",
    )(idx, *pieces, weights, grad)


def input_parts(idx, slopes, weights, extra):
    return pl.pallas_call(
        input_kernel,
        grid_spec=pltpu.PrefetchScalarGridSpec(
            num_scalar_prefetch=1,
            grid=(4,),
            in_specs=[
                _still(2 * TOK, UNITS),
                *[
                    pl.BlockSpec((BLK, UNITS), lambda k, i, q=q: (i[4 * k + q], 0))
                    for q in range(4)
                ],
                _still(2, EXTRA, BLK),
            ],
            out_specs=[
                pl.BlockSpec((1, 4, ROWS_A, BLK), lambda k, i: (k // 2, k % 2, 0, 0)),
                pl.BlockSpec((1, 4, ROWS_A, BLK), lambda k, i: (i[18 + k // 2], k % 2, 0, 0)),
                pl.BlockSpec((4, 2, ROWS_B, BLK), lambda k, i: (k % 2, k // 2, 0, 0)),
            ],
        ),
        out_shape=[
            jax.ShapeDtypeStruct((2, NZ, ROWS_A, BLK), BF),
            jax.ShapeDtypeStruct((2, NZ, ROWS_A, BLK), BF),
            jax.ShapeDtypeStruct((NZ, NY, ROWS_B, BLK), BF),
        ],
        compiler_params=_params(1),
        cost_estimate=_cost(2 * 640 * FEATS * UNITS, 14 << 20),
        name="input_parts",
    )(idx, slopes, *[weights] * 4, extra)


def weight_parts(idx, scaled, ready, before):
    return pl.pallas_call(
        weight_kernel,
        grid_spec=pltpu.PrefetchScalarGridSpec(
            num_scalar_prefetch=1,
            grid=(2,),
            in_specs=[
                *[
                    pl.BlockSpec((2 * TOK, BLK), lambda s, i, q=q: (0, i[4 * s + q]))
                    for q in range(4)
                ],
                _still(2 * TOK, UNITS),
                pl.BlockSpec(memory_space=pl.ANY),
            ],
            out_specs=pl.BlockSpec((4, BLK, UNITS), lambda s, i: (s, 0, 0)),
        ),
        out_shape=jax.ShapeDtypeStruct((8, BLK, UNITS), BF),
        compiler_params=_params(1),
        cost_estimate=_cost(640 * FEATS * UNITS, 7 << 20),
        name="weight_parts",
    )(idx, *[scaled] * 4, ready, before)


def gather_plane(shard, gain):
    high = gain.astype(BF)
    low = (gain - high.astype(F32)).astype(BF)
    head = jnp.concatenate([high[None], low[None], jnp.zeros((EXTRA - 2, BLK), BF)], axis=0)
    part_a = jnp.concatenate([head, shard[:TOK_A]], axis=0)
    part_b = shard[TOK_A:]
    half = NZ // 2
    b1, b3, b2 = move(part_b, flip=1), move(part_b, flip=3), move(part_b, flip=2)
    rows = {0: jnp.stack([part_b, b1, b2, b3])}
    line = {0: part_a}
    for p in (1, 2, 3):
        line[p], line[8 - p] = move(line[p - 1], dz=-1), move(line[(9 - p) % 8], dz=1)
    line[4] = move(part_a, dz=4)
    for p in (1, 2, 3):
        rows[p], rows[8 - p] = move(rows[p - 1], dz=-1), move(rows[(9 - p) % 8], dz=1)
    rows_4 = [move(rows[3][:2], dz=-1), move(rows[5][2:], dz=1)]
    a0 = jnp.stack([line[p] for p in range(NZ)])
    a1, a3 = move(a0, flip=1), move(a0, flip=3)
    a2 = [move(a1[:half], flip=3), move(a3[half:], flip=1)]
    return [a0, a1, *a2, a3, rows[0], rows[1], rows[2], rows[3], *rows_4, rows[5], rows[6], rows[7]]


def scatter_plane(own_a, par_a, part_b, d):
    part_a = own_a[0], par_a[0], own_a[1], par_a[1]
    around = move(part_a[3], dy=1, turn=True)
    for k in (2, 1):
        around = move(add(part_a[k], around).astype(BF), dy=1, turn=True)
    up, down = move(part_b[4, :2], dz=1), move(part_b[4, 2:], dz=-1)
    up = jnp.concatenate([add(part_b[3, :2], up).astype(BF), part_b[3, 2:]], axis=0)
    down = jnp.concatenate([part_b[5, :2], add(part_b[5, 2:], down).astype(BF)], axis=0)
    up, down = move(up, dz=1), move(down, dz=-1)
    for p in (2, 1):
        up = move(add(part_b[p], up).astype(BF), dz=1)
        down = move(add(part_b[8 - p], down).astype(BF), dz=-1)
    line = add(part_a[0], around)
    sent = line.astype(BF)
    sum_a = add(line[0], *[move(sent[p], dz=p) for p in (4, 3, 5, 2, 6, 1, 7)])
    column = add(part_b[0], up, down)
    sent = column.astype(BF)
    next_1, next_3 = pick(sent[1], sent[3], d), pick(sent[3], sent[1], d)
    sum_b = add(column[0], move(next_1, dy=1), move(next_3, dy=3), move(sent[2], dy=2))
    return sum_a, sum_b


def pick(first, second, d):
    return jnp.where(d == 0, first, second)


def mine(left, right, d):
    rest = FULL + 2 * HALF
    return jnp.concatenate(
        [
            pick(left[:, :FULL], left[:, rest:], d),
            pick(left[:, FULL : FULL + HALF], left[:, FULL + HALF : rest], d),
            pick(right[:, FULL : FULL + HALF], right[:, FULL + HALF : rest], d),
            pick(right[:, :FULL], right[:, rest:], d),
        ],
        axis=1,
    )


def tables():
    tensor, fsdp, d = (lax.axis_index(axis).astype(jnp.int32) for axis in AXES)
    y_hi, z = tensor // NZ, tensor % NZ
    x, c = fsdp // 2, fsdp % 2
    k = jnp.arange(16, dtype=jnp.int32)
    block = ((y_hi + k // 8) % 2) * NZ + (z + k % 8) % NZ
    partner = jnp.stack([1 + 2 * d, 3 - 2 * d])
    slot = jnp.where(c == 0, partner // 2, 1 - partner // 2)
    first = jnp.concatenate([block, jnp.zeros((2,), jnp.int32), slot])

    def of_core(core):
        s = jnp.arange(8, dtype=jnp.int32)
        to = x + (1 - 2 * core) * (s // 2)
        g = ((to % NX) * 2 + core) * 2 + s % 2
        h, p = (g // NZ - y_hi) % 2, (g % NZ - z) % NZ
        return h * NZ + p

    return block, first, of_core(1 - c), of_core(c), d


def body(inputs, norm_gain, gate_weight, up_weight, hidden_grad):
    block, first, other_core, this_core, d = tables()
    weights = lax.all_gather(mine(gate_weight, up_weight, d), "fsdp", axis=0, tiled=True)

    grad = hidden_grad[0]
    keep = mine(grad, grad, d)[:, : FULL + 128]
    give = mine(grad, grad, 1 - d)[:, : FULL + 128]
    grads = jnp.concatenate([keep, move(give, flip=1)], axis=0)

    local_x = inputs[0]
    pieces = gather_plane(local_x, norm_gain)
    scaled, slopes, ready, corr, inverse = forward(block, pieces, weights, grads)

    rows = jnp.pad(corr.reshape(2, TOK) / FEATS, ((0, 0), (0, 512 - TOK))).reshape(2, 2, BLK)
    extra = jnp.pad(rows, ((0, 0), (0, EXTRA - 2), (0, 0))).astype(BF)
    own_a, par_a, part_b = input_parts(first, slopes, weights, extra)

    theirs = weight_parts(other_core, scaled, ready, own_a)
    got = move(theirs, dc=1)
    ours = weight_parts(this_core, scaled, ready, theirs)

    sum_a, sum_b = scatter_plane(own_a, par_a, part_b, d)

    around = move(add(ours[6:], got[6:]).astype(BF), dx=1, turn=True)
    for k in (2, 1):
        part = slice(2 * k, 2 * k + 2)
        around = move(add(ours[part], got[part], around).astype(BF), dx=1, turn=True)
    rows_0, rows_1 = (add(ours[i], got[i], around[i]) for i in range(2))
    keep = pick(rows_0, rows_1, d).astype(BF)
    got = move(pick(rows_1, rows_0, d).astype(BF), flip=1)

    def whole(start, shared):
        left, right = pick(keep, got, d), pick(got, keep, d)
        return jnp.concatenate(
            [
                left[:, start : start + FULL],
                left[:, shared : shared + HALF],
                right[:, shared : shared + HALF],
                right[:, start : start + FULL],
            ],
            axis=1,
        )

    gate_grad = whole(0, FULL)
    up_grad = whole(FULL + 128, FULL + HALF)

    normed_grad = jnp.concatenate([sum_a[EXTRA:], sum_b], axis=0)
    correction = sum_a[:2].reshape(512)[:TOK][:, None]
    inv = inverse[:TOK]
    x = local_x.astype(F32)
    input_grad = inv * (normed_grad * norm_gain) - x * inv * inv * inv * correction
    gain_part = jnp.sum(normed_grad * x * inv, axis=0).reshape(2, 128)
    gain_part = gain_part + move(gain_part, dc=1)
    gain_part = (
        gain_part + move(gain_part, dx=1) + move(gain_part, dx=-1) + move(gain_part, dx=2)
    )
    gain_grad = (gain_part + move(gain_part, flip=1)).reshape(BLK)
    return input_grad.astype(BF)[None], gain_grad, gate_grad, up_grad


def solution(mesh):
    placed = (
        P(("fsdp", "dp"), None, "tensor"),
        P("tensor"),
        P("fsdp", "tensor"),
        P("fsdp", "tensor"),
        P(("fsdp", "dp"), None, "tensor"),
    )
    return jax.shard_map(
        body,
        mesh=mesh,
        in_specs=placed,
        out_specs=(
            P(("fsdp", "dp"), None, "tensor"),
            P("tensor"),
            P(("fsdp", "dp"), "tensor"),
            P(("fsdp", "dp"), "tensor"),
        ),
        check_vma=False,
    )
```

```python
import jax
import jax.numpy as jnp
from jax import lax
from jax.experimental import pallas as pl
from jax.experimental.pallas import tpu as pltpu
from jax.sharding import PartitionSpec as P

norm_epsilon = 1e-05
AXES = ("tensor", "fsdp", "dp")
NX, NY, NZ = 4, 4, 8
BF = jnp.bfloat16
F32 = jnp.float32
TOK = 320
BLK = 256
FEATS = 4096
UNITS = 896
EXTRA = 16
IN_A = 160
OUT_A = 128
CUT = 96
FULL = 384
HALF = 64


def _index(x, c, y, z):
    return (((y % NY) // 2) * NZ + z % NZ) * 16 + ((x % NX) * 2 + c % 2) * 2 + y % 2


def _pairs(dx=0, dc=0, dy=0, dz=0, flip=0, turn=False):
    pairs = []
    for x in range(NX):
        for c in range(2):
            way = -1 if turn and c else 1
            for y in range(NY):
                for z in range(NZ):
                    to = (y ^ flip) + way * dy
                    there = _index(x + way * dx, c + dc, to, z + way * dz)
                    pairs.append((_index(x, c, y, z), there))
    return pairs


def move(value, **step):
    return lax.ppermute(value, AXES, _pairs(**step))


def swap_z(blocks):
    lines = [[half * NZ + z for z in range(NZ)] for half in range(2)]
    return lax.all_to_all(
        blocks, "tensor", split_axis=0, concat_axis=0, tiled=True, axis_index_groups=lines
    )


def after(value, *others):
    return lax.optimization_barrier((value, *others))[0]


def add(*terms):
    total = terms[0].astype(F32)
    for term in terms[1:]:
        total = total + term.astype(F32)
    return total


CHUNK = 64


def forward_kernel(idx, *refs):
    line, twin, upper, lower, cross = refs[:5]
    pieces_a = ([line], [twin], [upper, lower], [cross])
    pieces_b = refs[5:13]
    w, grad, scaled, slopes, ready, corr, inverse, acc, square, held, sems = refs[13:]

    def fetch(k):
        there = pl.ds(pl.multiple_of(idx[k] * BLK, BLK), BLK)
        return pltpu.make_async_copy(w.at[there], held.at[pl.ds(k * BLK, BLK)], sems.at[k])

    for k in range(16):
        fetch(k).start()
    square[...] = jnp.zeros_like(square)
    for group in range(4):
        h, quad = group // 2, group % 2
        for m in range(2):
            j = 2 * h + m
            sums_a, sums_b = [], []
            for q in range(4):
                p = 4 * quad + q
                lanes = pl.ds((4 * group + q) * BLK, BLK)
                at = lax.rem(idx[8 * h + p], NZ)
                head = pieces_a[j][0][at, 0:EXTRA, :].astype(F32)
                gain = head[0:1] + head[1:2]
                row, skip = m * TOK, EXTRA
                for piece in pieces_a[j]:
                    x = piece[at, skip:, :].astype(F32)
                    scaled[pl.ds(row, x.shape[0]), lanes] = (x * gain).astype(BF)
                    sq = x * x
                    sums_a.append((row, sq[:, :128] + sq[:, 128:]))
                    row, skip = row + x.shape[0], 0
                x = pieces_b[p][j].astype(F32)
                scaled[pl.ds(m * TOK + IN_A, TOK - IN_A), lanes] = (x * gain).astype(BF)
                sq = x * x
                sums_b.append(sq[:, :128] + sq[:, 128:])
            for row in sorted({row for row, _ in sums_a}):
                terms = [sq for at, sq in sums_a if at == row]
                square[pl.ds(row, terms[0].shape[0]), :] += sum(terms[1:], terms[0])
            square[pl.ds(m * TOK + IN_A, TOK - IN_A), :] += sum(sums_b[1:], sums_b[0])
        for q in range(4):
            fetch(4 * group + q).wait()
        lanes = pl.ds(4 * group * BLK, 4 * BLK)
        product = jnp.dot(scaled[:, lanes], held[lanes, :], preferred_element_type=F32)
        acc[...] = product if group == 0 else acc[...] + product

    first = lax.broadcasted_iota(jnp.int32, (CHUNK, 128), 1) < HALF

    def slope_pair(gate, up, upstream):
        s = 1.0 / (1.0 + jnp.exp(-gate))
        return upstream * up * s * (1.0 + gate * (1.0 - s)), upstream * gate * s

    for chunk in range(2 * TOK // CHUNK):
        rows = pl.ds(chunk * CHUNK, CHUNK)
        mean = jnp.sum(square[rows, :], axis=-1, keepdims=True) / FEATS
        inv = lax.rsqrt(mean + norm_epsilon)
        total = jnp.zeros((CHUNK, 128), F32)
        for tile in range(FULL // 128):
            here, there = pl.ds(tile * 128, 128), pl.ds(FULL + 128 + tile * 128, 128)
            gate, up = acc[rows, here] * inv, acc[rows, there] * inv
            down, lift = slope_pair(gate, up, grad[rows, here].astype(F32))
            slopes[rows, here] = down.astype(BF)
            slopes[rows, there] = lift.astype(BF)
            ready[rows, here] = (down * inv).astype(BF)
            ready[rows, there] = (lift * inv).astype(BF)
            total += down * gate + lift * up
        here = pl.ds(FULL, 128)
        mixed = acc[rows, here] * inv
        turned = pltpu.roll(mixed, HALF, 1)
        gate, up = jnp.where(first, mixed, turned), jnp.where(first, turned, mixed)
        down, lift = slope_pair(gate, up, grad[rows, here].astype(F32))
        both = jnp.where(first, down, lift)
        slopes[rows, here] = both.astype(BF)
        ready[rows, here] = (both * inv).astype(BF)
        total += both * mixed
        corr[rows, :] = jnp.sum(total, axis=-1, keepdims=True) / inv
        inverse[rows, :] = inv


def input_kernel(idx, slopes, w0, w1, w2, w3, extra, before, own_a, par_a, out_b):
    step = pl.program_id(0)
    for q, w in enumerate((w0, w1, w2, w3)):
        part = lax.dot_general(
            slopes[...], w[...], (((1,), (1,)), ((), ())), preferred_element_type=F32
        ).astype(BF)
        at = lax.rem(idx[4 * step + q], NZ)
        for m, out_a in enumerate((own_a, par_a)):
            out_a[0, at, :EXTRA, :] = extra[m]
            out_a[0, at, EXTRA:, :] = part[m * TOK : m * TOK + OUT_A]
            out_b[q, m] = part[m * TOK + OUT_A : (m + 1) * TOK]


def weight_kernel(idx, x0, x1, x2, x3, ready, before, out):
    for q, x in enumerate((x0, x1, x2, x3)):
        out[q] = lax.dot_general(
            x[...], ready[...], (((0,), (0,)), ((), ())), preferred_element_type=F32
        ).astype(BF)


LIMIT = 56 * 1024 * 1024


def _params(dims):
    return pltpu.CompilerParams(
        dimension_semantics=("arbitrary",) * dims, vmem_limit_bytes=LIMIT
    )


def _cost(flops, moved, exps=0):
    return pl.CostEstimate(flops=flops, bytes_accessed=moved, transcendentals=exps)


def _still(*shape):
    return pl.BlockSpec(shape, lambda *_: (0,) * len(shape))


def forward(idx, pieces, weights, grad):
    smem = pl.BlockSpec(memory_space=pltpu.SMEM)
    vmem = pl.BlockSpec(memory_space=pltpu.VMEM)
    return pl.pallas_call(
        forward_kernel,
        in_specs=[smem, *[vmem] * 13, pl.BlockSpec(memory_space=pl.ANY), vmem],
        out_specs=[vmem] * 5,
        scratch_shapes=[
            pltpu.VMEM((2 * TOK, UNITS), F32),
            pltpu.VMEM((2 * TOK, 128), F32),
            pltpu.VMEM((FEATS, UNITS), BF),
            pltpu.SemaphoreType.DMA((16,)),
        ],
        out_shape=[
            jax.ShapeDtypeStruct((2 * TOK, FEATS), BF),
            jax.ShapeDtypeStruct((2 * TOK, UNITS), BF),
            jax.ShapeDtypeStruct((2 * TOK, UNITS), BF),
            jax.ShapeDtypeStruct((2 * TOK, 1), F32),
            jax.ShapeDtypeStruct((2 * TOK, 1), F32),
        ],
        compiler_params=pltpu.CompilerParams(vmem_limit_bytes=LIMIT),
        cost_estimate=_cost(2 * 640 * FEATS * UNITS, 14 << 20, 640 * 512),
        name="forward_slopes",
    )(idx, *pieces, weights, grad)


def input_parts(idx, slopes, weights, extra, before):
    return pl.pallas_call(
        input_kernel,
        grid_spec=pltpu.PrefetchScalarGridSpec(
            num_scalar_prefetch=1,
            grid=(4,),
            in_specs=[
                _still(2 * TOK, UNITS),
                *[
                    pl.BlockSpec((BLK, UNITS), lambda k, i, q=q: (i[4 * k + q], 0))
                    for q in range(4)
                ],
                _still(2, EXTRA, BLK),
                pl.BlockSpec(memory_space=pl.ANY),
            ],
            out_specs=[
                pl.BlockSpec((1, NZ, EXTRA + OUT_A, BLK), lambda k, i: (k // 2, 0, 0, 0)),
                pl.BlockSpec((1, NZ, EXTRA + OUT_A, BLK), lambda k, i: (i[16 + k // 2], 0, 0, 0)),
                pl.BlockSpec((4, 2, TOK - OUT_A, BLK), lambda k, i: (k % 2, k // 2, 0, 0)),
            ],
        ),
        out_shape=[
            *[jax.ShapeDtypeStruct((2, NZ, EXTRA + OUT_A, BLK), BF)] * 2,
            jax.ShapeDtypeStruct((NZ, 4, TOK - OUT_A, BLK), BF),
        ],
        compiler_params=_params(1),
        cost_estimate=_cost(2 * 640 * FEATS * UNITS, 14 << 20),
        name="input_parts",
    )(idx, slopes, *[weights] * 4, extra, before)


def weight_parts(idx, scaled, ready, before):
    return pl.pallas_call(
        weight_kernel,
        grid_spec=pltpu.PrefetchScalarGridSpec(
            num_scalar_prefetch=1,
            grid=(2,),
            in_specs=[
                *[
                    pl.BlockSpec((2 * TOK, BLK), lambda s, i, q=q: (0, i[4 * s + q]))
                    for q in range(4)
                ],
                _still(2 * TOK, UNITS),
                pl.BlockSpec(memory_space=pl.ANY),
            ],
            out_specs=pl.BlockSpec((4, BLK, UNITS), lambda s, i: (s, 0, 0)),
        ),
        out_shape=jax.ShapeDtypeStruct((8, BLK, UNITS), BF),
        compiler_params=_params(1),
        cost_estimate=_cost(640 * FEATS * UNITS, 7 << 20),
        name="weight_parts",
    )(idx, *[scaled] * 4, ready, before)


def gather_plane(shard, gain, pair):
    high = gain.astype(BF)
    low = (gain - high.astype(F32)).astype(BF)
    head = jnp.concatenate([high[None], low[None], jnp.zeros((EXTRA - 2, BLK), BF)], axis=0)
    part_a = jnp.concatenate([head, shard[:IN_A]], axis=0)
    part_b = shard[IN_A:]
    rows = {0: jnp.stack([part_b] + [move(part_b, flip=j) for j in (1, 2, 3)])}
    line = swap_z(jnp.broadcast_to(part_a, (NZ, *part_a.shape)))
    rows[1], rows[7] = move(rows[0], dz=-1, turn=True), move(rows[0], dz=1, turn=True)
    line = after(line, pair)
    twin, cross = move(line, flip=1), move(line, flip=3)
    rows[1], rows[7] = after((rows[1], rows[7]), line)
    for p in (2, 3):
        rows[p] = move(rows[p - 1], dz=-1, turn=True)
        rows[8 - p] = move(rows[(9 - p) % 8], dz=1, turn=True)
    rows[4] = move(rows[3], dz=-1, turn=True)
    upper, lower = move(twin[:, :CUT], flip=3), move(cross[:, CUT:], flip=1)
    return [line, twin, upper, lower, cross] + [rows[p] for p in range(NZ)]


def pick(first, second, d):
    return jnp.where(d == 0, first, second)


def mine(left, right, d):
    rest = FULL + 2 * HALF
    return jnp.concatenate(
        [
            pick(left[:, :FULL], left[:, rest:], d),
            pick(left[:, FULL : FULL + HALF], left[:, FULL + HALF : rest], d),
            pick(right[:, FULL : FULL + HALF], right[:, FULL + HALF : rest], d),
            pick(right[:, :FULL], right[:, rest:], d),
        ],
        axis=1,
    )


def tables():
    tensor, fsdp, d = (lax.axis_index(axis).astype(jnp.int32) for axis in AXES)
    y_hi, z = tensor // NZ, tensor % NZ
    x, c = fsdp // 2, fsdp % 2
    k = jnp.arange(16, dtype=jnp.int32)
    block = ((y_hi + k // 8) % 2) * NZ + (z + (1 - 2 * c) * (k % 8)) % NZ
    order = jnp.concatenate([block, jnp.stack([d ^ c, 1 - (d ^ c)])])

    def of_core(core):
        s = jnp.arange(8, dtype=jnp.int32)
        to = x + (1 - 2 * core) * (s // 2)
        g = ((to % NX) * 2 + core) * 2 + s % 2
        h, p = (g // NZ - y_hi) % 2, ((1 - 2 * c) * (g % NZ - z)) % NZ
        return h * NZ + p

    return block, order, of_core(1 - c), of_core(c), d


def body(inputs, norm_gain, gate_weight, up_weight, hidden_grad):
    block, order, other_core, this_core, d = tables()
    weights = lax.all_gather(mine(gate_weight, up_weight, d), "fsdp", axis=0, tiled=True)

    grad = hidden_grad[0]
    keep = mine(grad, grad, d)[:, : FULL + 128]
    give = mine(grad, grad, 1 - d)[:, : FULL + 128]
    received = move(give, flip=1)
    grads = jnp.concatenate([keep, received], axis=0)

    local_x = inputs[0]
    pieces = gather_plane(local_x, norm_gain, received)
    scaled, slopes, ready, corr, inverse = forward(block, pieces, weights, grads)

    rows = jnp.pad(corr.reshape(2, TOK) / FEATS, ((0, 0), (0, 512 - TOK))).reshape(2, 2, BLK)
    extra = jnp.pad(rows, ((0, 0), (0, EXTRA - 2), (0, 0))).astype(BF)
    theirs = weight_parts(other_core, scaled, ready, ready)
    got = move(theirs, dc=1)
    own_a, par_a, part_b = input_parts(order, slopes, weights, extra, theirs)

    ring_y = move(par_a[1], dy=1, turn=True)
    up = move(part_b[4], dz=1, turn=True)
    ours = weight_parts(this_core, scaled, ready, part_b)
    parts = [add(ours[2 * k : 2 * k + 2], got[2 * k : 2 * k + 2]) for k in range(NX)]

    ring_y = add(own_a[1], ring_y).astype(BF)
    up, down = add(part_b[3], up).astype(BF), part_b[5]
    ring_y, up, down = after((ring_y, up, down), ours)
    ring_y = move(ring_y, dy=1, turn=True)
    up, down = move(up, dz=1, turn=True), move(down, dz=-1, turn=True)
    x_next = move(parts[1].astype(BF), dx=1, turn=True)

    ring_y = add(par_a[0], ring_y).astype(BF)
    up, down = add(part_b[2], up).astype(BF), add(part_b[6], down).astype(BF)
    ring_y, up, down = after((ring_y, up, down), x_next)
    ring_y = move(ring_y, dy=1, turn=True)
    up, down = move(up, dz=1, turn=True), move(down, dz=-1, turn=True)
    x_across = move(after(parts[2].astype(BF), x_next), dx=2)

    line = add(own_a[0], ring_y).astype(BF)
    up, down = add(part_b[1], up).astype(BF), add(part_b[7], down).astype(BF)
    line, up, down, last = after((line, up, down, parts[3].astype(BF)))
    up, down = move(up, dz=1, turn=True), move(down, dz=-1, turn=True)
    line = swap_z(line)
    x_back = move(last, dx=-1, turn=True)

    column, x_across = after((add(part_b[0], up, down), x_across))
    sent = column.astype(BF)
    sum_b = add(column[0], *[move(sent[j], flip=j) for j in (1, 2, 3)])
    sum_a = jnp.sum(after(line, x_back).astype(F32), axis=0)
    rows = add(parts[0], x_next, x_across, x_back)
    rows_0, rows_1 = rows[0], rows[1]
    keep = pick(rows_0, rows_1, d).astype(BF)
    got = move(pick(rows_1, rows_0, d).astype(BF), flip=1)

    def whole(start, shared):
        left, right = pick(keep, got, d), pick(got, keep, d)
        return jnp.concatenate(
            [
                left[:, start : start + FULL],
                left[:, shared : shared + HALF],
                right[:, shared : shared + HALF],
                right[:, start : start + FULL],
            ],
            axis=1,
        )

    gate_grad = whole(0, FULL)
    up_grad = whole(FULL + 128, FULL + HALF)

    normed_grad = jnp.concatenate([sum_a[EXTRA:], sum_b], axis=0)
    correction = sum_a[:2].reshape(512)[:TOK][:, None]
    inv = inverse[:TOK]
    x = local_x.astype(F32)
    input_grad = inv * (normed_grad * norm_gain) - x * inv * inv * inv * correction
    gain_part = jnp.sum(normed_grad * x * inv, axis=0).reshape(2, 128)
    gain_part = gain_part + move(gain_part, dc=1)
    gain_part = (
        gain_part + move(gain_part, dx=1) + move(gain_part, dx=-1) + move(gain_part, dx=2)
    )
    gain_grad = (gain_part + move(gain_part, flip=1)).reshape(BLK)
    return input_grad.astype(BF)[None], gain_grad, gate_grad, up_grad


def solution(mesh):
    placed = (
        P(("fsdp", "dp"), None, "tensor"),
        P("tensor"),
        P("fsdp", "tensor"),
        P("fsdp", "tensor"),
        P(("fsdp", "dp"), None, "tensor"),
    )
    return jax.shard_map(
        body,
        mesh=mesh,
        in_specs=placed,
        out_specs=(
            P(("fsdp", "dp"), None, "tensor"),
            P("tensor"),
            P(("fsdp", "dp"), "tensor"),
            P(("fsdp", "dp"), "tensor"),
        ),
        check_vma=False,
    )
```

```python
import jax
import jax.numpy as jnp
from jax import lax
from jax.experimental import pallas as pl
from jax.experimental.pallas import tpu as pltpu
from jax.sharding import PartitionSpec as P

norm_epsilon = 1e-05
AXES = ("tensor", "fsdp", "dp")
NX, NY, NZ = 4, 4, 8
BF = jnp.bfloat16
F32 = jnp.float32
TOK = 320
BLK = 256
FEATS = 4096
UNITS = 896
EXTRA = 16
IN_A = 160
OUT_A = 128
CUT = 96
FULL = 384
HALF = 64


def _index(x, c, y, z):
    return (((y % NY) // 2) * NZ + z % NZ) * 16 + ((x % NX) * 2 + c % 2) * 2 + y % 2


def _pairs(dx=0, dc=0, dy=0, dz=0, flip=0, turn=False):
    pairs = []
    for x in range(NX):
        for c in range(2):
            way = -1 if turn and c else 1
            for y in range(NY):
                for z in range(NZ):
                    to = (y ^ flip) + way * dy
                    there = _index(x + way * dx, c + dc, to, z + way * dz)
                    pairs.append((_index(x, c, y, z), there))
    return pairs


def move(value, **step):
    return lax.ppermute(value, AXES, _pairs(**step))


def swap_z(blocks):
    lines = [[half * NZ + z for z in range(NZ)] for half in range(2)]
    return lax.all_to_all(
        blocks, "tensor", split_axis=0, concat_axis=0, tiled=True, axis_index_groups=lines
    )


def after(value, *others):
    return lax.optimization_barrier((value, *others))[0]


def add(*terms):
    total = terms[0].astype(F32)
    for term in terms[1:]:
        total = total + term.astype(F32)
    return total


CHUNK = 64


def forward_kernel(idx, *refs):
    line, twin, upper, lower, cross = refs[:5]
    pieces_a = ([line], [twin], [upper, lower], [cross])
    pieces_b = refs[5:13]
    w, grad, scaled, slopes, ready, corr, inverse, acc, square, held, sems = refs[13:]

    def fetch(k):
        there = pl.ds(pl.multiple_of(idx[k] * BLK, BLK), BLK)
        return pltpu.make_async_copy(w.at[there], held.at[pl.ds(k * BLK, BLK)], sems.at[k])

    for k in range(16):
        fetch(k).start()
    square[...] = jnp.zeros_like(square)
    for group in range(4):
        h, quad = group // 2, group % 2
        for m in range(2):
            j = 2 * h + m
            sums_a, sums_b = [], []
            for q in range(4):
                p = 4 * quad + q
                lanes = pl.ds((4 * group + q) * BLK, BLK)
                at = lax.rem(idx[8 * h + p], NZ)
                head = pieces_a[j][0][at, 0:EXTRA, :].astype(F32)
                gain = head[0:1] + head[1:2]
                row, skip = m * TOK, EXTRA
                for piece in pieces_a[j]:
                    x = piece[at, skip:, :].astype(F32)
                    scaled[pl.ds(row, x.shape[0]), lanes] = (x * gain).astype(BF)
                    sq = x * x
                    sums_a.append((row, sq[:, :128] + sq[:, 128:]))
                    row, skip = row + x.shape[0], 0
                x = pieces_b[p][j].astype(F32)
                scaled[pl.ds(m * TOK + IN_A, TOK - IN_A), lanes] = (x * gain).astype(BF)
                sq = x * x
                sums_b.append(sq[:, :128] + sq[:, 128:])
            for row in sorted({row for row, _ in sums_a}):
                terms = [sq for at, sq in sums_a if at == row]
                square[pl.ds(row, terms[0].shape[0]), :] += sum(terms[1:], terms[0])
            square[pl.ds(m * TOK + IN_A, TOK - IN_A), :] += sum(sums_b[1:], sums_b[0])
        for q in range(4):
            fetch(4 * group + q).wait()
        lanes = pl.ds(4 * group * BLK, 4 * BLK)
        product = jnp.dot(scaled[:, lanes], held[lanes, :], preferred_element_type=F32)
        acc[...] = product if group == 0 else acc[...] + product

    first = lax.broadcasted_iota(jnp.int32, (CHUNK, 128), 1) < HALF

    def slope_pair(gate, up, upstream):
        s = 1.0 / (1.0 + jnp.exp(-gate))
        return upstream * up * s * (1.0 + gate * (1.0 - s)), upstream * gate * s

    for chunk in range(2 * TOK // CHUNK):
        rows = pl.ds(chunk * CHUNK, CHUNK)
        mean = jnp.sum(square[rows, :], axis=-1, keepdims=True) / FEATS
        inv = lax.rsqrt(mean + norm_epsilon)
        total = jnp.zeros((CHUNK, 128), F32)
        for tile in range(FULL // 128):
            here, there = pl.ds(tile * 128, 128), pl.ds(FULL + 128 + tile * 128, 128)
            gate, up = acc[rows, here] * inv, acc[rows, there] * inv
            down, lift = slope_pair(gate, up, grad[rows, here].astype(F32))
            slopes[rows, here] = down.astype(BF)
            slopes[rows, there] = lift.astype(BF)
            ready[rows, here] = (down * inv).astype(BF)
            ready[rows, there] = (lift * inv).astype(BF)
            total += down * gate + lift * up
        here = pl.ds(FULL, 128)
        mixed = acc[rows, here] * inv
        turned = pltpu.roll(mixed, HALF, 1)
        gate, up = jnp.where(first, mixed, turned), jnp.where(first, turned, mixed)
        down, lift = slope_pair(gate, up, grad[rows, here].astype(F32))
        both = jnp.where(first, down, lift)
        slopes[rows, here] = both.astype(BF)
        ready[rows, here] = (both * inv).astype(BF)
        total += both * mixed
        corr[rows, :] = jnp.sum(total, axis=-1, keepdims=True) / inv
        inverse[rows, :] = inv


def input_kernel(idx, slopes, w0, w1, w2, w3, extra, before, own_a, par_a, out_b):
    step = pl.program_id(0)
    for q, w in enumerate((w0, w1, w2, w3)):
        part = lax.dot_general(
            slopes[...], w[...], (((1,), (1,)), ((), ())), preferred_element_type=F32
        ).astype(BF)
        at = lax.rem(idx[4 * step + q], NZ)
        for m, out_a in enumerate((own_a, par_a)):
            out_a[0, at, :EXTRA, :] = extra[m]
            out_a[0, at, EXTRA:, :] = part[m * TOK : m * TOK + OUT_A]
            out_b[q, m] = part[m * TOK + OUT_A : (m + 1) * TOK]


def weight_kernel(idx, x0, x1, x2, x3, ready, *refs):
    got, out = refs[:-1], refs[-1]
    for q, x in enumerate((x0, x1, x2, x3)):
        part = lax.dot_general(
            x[...], ready[...], (((0,), (0,)), ((), ())), preferred_element_type=F32
        )
        out[q] = (part + got[0][q].astype(F32) if got else part).astype(BF)


MIB = 1024 * 1024


def _params():
    return pltpu.CompilerParams(dimension_semantics=("arbitrary",), vmem_limit_bytes=22 * MIB)


def _cost(flops, moved, exps=0):
    return pl.CostEstimate(flops=flops, bytes_accessed=moved, transcendentals=exps)


def _still(*shape):
    return pl.BlockSpec(shape, lambda *_: (0,) * len(shape))


def forward(idx, pieces, weights, grad):
    smem = pl.BlockSpec(memory_space=pltpu.SMEM)
    vmem = pl.BlockSpec(memory_space=pltpu.VMEM)
    return pl.pallas_call(
        forward_kernel,
        in_specs=[smem, *[vmem] * 13, pl.BlockSpec(memory_space=pl.ANY), vmem],
        out_specs=[vmem] * 5,
        scratch_shapes=[
            pltpu.VMEM((2 * TOK, UNITS), F32),
            pltpu.VMEM((2 * TOK, 128), F32),
            pltpu.VMEM((FEATS, UNITS), BF),
            pltpu.SemaphoreType.DMA((16,)),
        ],
        out_shape=[
            jax.ShapeDtypeStruct((2 * TOK, FEATS), BF),
            jax.ShapeDtypeStruct((2 * TOK, UNITS), BF),
            jax.ShapeDtypeStruct((2 * TOK, UNITS), BF),
            jax.ShapeDtypeStruct((2 * TOK, 1), F32),
            jax.ShapeDtypeStruct((2 * TOK, 1), F32),
        ],
        compiler_params=pltpu.CompilerParams(vmem_limit_bytes=34 * MIB),
        cost_estimate=_cost(2 * 640 * FEATS * UNITS, 14 << 20, 640 * 512),
        name="forward_slopes",
    )(idx, *pieces, weights, grad)


def input_parts(idx, slopes, weights, extra, before):
    return pl.pallas_call(
        input_kernel,
        grid_spec=pltpu.PrefetchScalarGridSpec(
            num_scalar_prefetch=1,
            grid=(4,),
            in_specs=[
                _still(2 * TOK, UNITS),
                *[
                    pl.BlockSpec((BLK, UNITS), lambda k, i, q=q: (i[4 * k + q], 0))
                    for q in range(4)
                ],
                _still(2, EXTRA, BLK),
                pl.BlockSpec(memory_space=pl.ANY),
            ],
            out_specs=[
                pl.BlockSpec((1, NZ, EXTRA + OUT_A, BLK), lambda k, i: (k // 2, 0, 0, 0)),
                pl.BlockSpec((1, NZ, EXTRA + OUT_A, BLK), lambda k, i: (i[16 + k // 2], 0, 0, 0)),
                pl.BlockSpec((4, 2, TOK - OUT_A, BLK), lambda k, i: (k % 2, k // 2, 0, 0)),
            ],
        ),
        out_shape=[
            *[jax.ShapeDtypeStruct((2, NZ, EXTRA + OUT_A, BLK), BF)] * 2,
            jax.ShapeDtypeStruct((NZ, 4, TOK - OUT_A, BLK), BF),
        ],
        compiler_params=_params(),
        cost_estimate=_cost(2 * 640 * FEATS * UNITS, 14 << 20),
        name="input_parts",
    )(idx, slopes, *[weights] * 4, extra, before)


def weight_parts(idx, scaled, ready, *got):
    blocks = pl.BlockSpec((4, BLK, UNITS), lambda s, i: (s, 0, 0))
    return pl.pallas_call(
        weight_kernel,
        grid_spec=pltpu.PrefetchScalarGridSpec(
            num_scalar_prefetch=1,
            grid=(2,),
            in_specs=[
                *[
                    pl.BlockSpec((2 * TOK, BLK), lambda s, i, q=q: (0, i[4 * s + q]))
                    for q in range(4)
                ],
                _still(2 * TOK, UNITS),
                *[blocks] * len(got),
            ],
            out_specs=blocks,
        ),
        out_shape=jax.ShapeDtypeStruct((8, BLK, UNITS), BF),
        compiler_params=_params(),
        cost_estimate=_cost(640 * FEATS * UNITS, 7 << 20),
        name="weight_parts",
    )(idx, *[scaled] * 4, ready, *got)


def gather_plane(shard, gain, pair):
    high = gain.astype(BF)
    low = (gain - high.astype(F32)).astype(BF)
    head = jnp.concatenate([high[None], low[None], jnp.zeros((EXTRA - 2, BLK), BF)], axis=0)
    part_a = jnp.concatenate([head, shard[:IN_A]], axis=0)
    part_b = shard[IN_A:]
    rows = {0: jnp.stack([part_b] + [move(part_b, flip=j) for j in (1, 2, 3)])}
    line = swap_z(jnp.broadcast_to(part_a, (NZ, *part_a.shape)))
    rows[1], rows[7] = move(rows[0], dz=-1, turn=True), move(rows[0], dz=1, turn=True)
    line = after(line, pair)
    twin, cross = move(line, flip=1), move(line, flip=3)
    rows[1], rows[7] = after((rows[1], rows[7]), line)
    for p in (2, 3):
        rows[p] = move(rows[p - 1], dz=-1, turn=True)
        rows[8 - p] = move(rows[(9 - p) % 8], dz=1, turn=True)
    rows[4] = move(rows[3], dz=-1, turn=True)
    upper, lower = move(twin[:, :CUT], flip=3), move(cross[:, CUT:], flip=1)
    return [line, twin, upper, lower, cross] + [rows[p] for p in range(NZ)]


def pick(first, second, d):
    return jnp.where(d == 0, first, second)


def mine(left, right, d):
    rest = FULL + 2 * HALF
    return jnp.concatenate(
        [
            pick(left[:, :FULL], left[:, rest:], d),
            pick(left[:, FULL : FULL + HALF], left[:, FULL + HALF : rest], d),
            pick(right[:, FULL : FULL + HALF], right[:, FULL + HALF : rest], d),
            pick(right[:, :FULL], right[:, rest:], d),
        ],
        axis=1,
    )


def tables():
    tensor, fsdp, d = (lax.axis_index(axis).astype(jnp.int32) for axis in AXES)
    y_hi, z = tensor // NZ, tensor % NZ
    x, c = fsdp // 2, fsdp % 2
    k = jnp.arange(16, dtype=jnp.int32)
    block = ((y_hi + k // 8) % 2) * NZ + (z + (1 - 2 * c) * (k % 8)) % NZ
    order = jnp.concatenate([block, jnp.stack([d ^ c, 1 - (d ^ c)])])

    def of_core(core):
        s = jnp.arange(8, dtype=jnp.int32)
        to = x + (1 - 2 * core) * (s // 2)
        g = ((to % NX) * 2 + core) * 2 + s % 2
        h, p = (g // NZ - y_hi) % 2, ((1 - 2 * c) * (g % NZ - z)) % NZ
        return h * NZ + p

    return block, order, of_core(1 - c), of_core(c), d


def body(inputs, norm_gain, gate_weight, up_weight, hidden_grad):
    block, order, other_core, this_core, d = tables()
    weights = lax.all_gather(mine(gate_weight, up_weight, d), "fsdp", axis=0, tiled=True)

    grad = hidden_grad[0]
    keep = mine(grad, grad, d)[:, : FULL + 128]
    give = mine(grad, grad, 1 - d)[:, : FULL + 128]
    received = move(give, flip=1)
    grads = jnp.concatenate([keep, received], axis=0)

    local_x = inputs[0]
    pieces = gather_plane(local_x, norm_gain, received)
    scaled, slopes, ready, corr, inverse = forward(block, pieces, weights, grads)

    rows = jnp.pad(corr.reshape(2, TOK) / FEATS, ((0, 0), (0, 512 - TOK))).reshape(2, 2, BLK)
    extra = jnp.pad(rows, ((0, 0), (0, EXTRA - 2), (0, 0))).astype(BF)
    theirs = weight_parts(other_core, scaled, ready)
    got = move(theirs, dc=1)
    own_a, par_a, part_b = input_parts(order, slopes, weights, extra, theirs)

    ring_y = move(par_a[1], dy=1, turn=True)
    up = move(part_b[4], dz=1, turn=True)
    ours = weight_parts(this_core, scaled, after(ready, part_b), got)
    parts = [ours[2 * k : 2 * k + 2] for k in range(NX)]

    ring_y, up = after((ring_y, up), ours)
    ring_y = add(own_a[1], ring_y).astype(BF)
    up, down = add(part_b[3], up).astype(BF), part_b[5]
    ring_y, up, down = after((ring_y, up, down))
    ring_y = move(ring_y, dy=1, turn=True)
    up, down = move(up, dz=1, turn=True), move(down, dz=-1, turn=True)
    x_next = move(parts[1], dx=1, turn=True)

    ring_y = add(par_a[0], ring_y).astype(BF)
    up, down = add(part_b[2], up).astype(BF), add(part_b[6], down).astype(BF)
    ring_y, up, down = after((ring_y, up, down))
    ring_y = move(ring_y, dy=1, turn=True)
    up, down = move(up, dz=1, turn=True), move(down, dz=-1, turn=True)

    line = add(own_a[0], ring_y).astype(BF)
    up, down = add(part_b[1], up).astype(BF), add(part_b[7], down).astype(BF)
    line, up, down, far_x, last_x = after((line, up, down, parts[2], parts[3]), x_next)
    up, down = move(up, dz=1, turn=True), move(down, dz=-1, turn=True)
    line = swap_z(line)
    x_across, x_back = move(far_x, dx=2), move(last_x, dx=-1, turn=True)

    column = add(part_b[0], up, down)
    sent = column.astype(BF)
    sum_b = add(column[0], *[move(sent[j], flip=j) for j in (1, 2, 3)])
    sum_a = jnp.sum(line.astype(F32), axis=0)
    x_across, x_back = after((x_across, x_back), sum_b)
    rows = add(parts[0], x_next, x_across, x_back)
    rows_0, rows_1 = rows[0], rows[1]
    keep = pick(rows_0, rows_1, d).astype(BF)
    got = move(pick(rows_1, rows_0, d).astype(BF), flip=1)

    def whole(start, shared):
        left, right = pick(keep, got, d), pick(got, keep, d)
        return jnp.concatenate(
            [
                left[:, start : start + FULL],
                left[:, shared : shared + HALF],
                right[:, shared : shared + HALF],
                right[:, start : start + FULL],
            ],
            axis=1,
        )

    gate_grad = whole(0, FULL)
    up_grad = whole(FULL + 128, FULL + HALF)

    normed_grad = jnp.concatenate([sum_a[EXTRA:], sum_b], axis=0)
    correction = sum_a[:2].reshape(512)[:TOK][:, None]
    inv = inverse[:TOK]
    x = local_x.astype(F32)
    input_grad = inv * (normed_grad * norm_gain) - x * inv * inv * inv * correction
    gain_part = jnp.sum(normed_grad * x * inv, axis=0).reshape(2, 128)
    gain_part = gain_part + move(gain_part, dc=1)
    gain_part = (
        gain_part + move(gain_part, dx=1) + move(gain_part, dx=-1) + move(gain_part, dx=2)
    )
    gain_grad = (gain_part + move(gain_part, flip=1)).reshape(BLK)
    return input_grad.astype(BF)[None], gain_grad, gate_grad, up_grad


def solution(mesh):
    placed = (
        P(("fsdp", "dp"), None, "tensor"),
        P("tensor"),
        P("fsdp", "tensor"),
        P("fsdp", "tensor"),
        P(("fsdp", "dp"), None, "tensor"),
    )
    return jax.shard_map(
        body,
        mesh=mesh,
        in_specs=placed,
        out_specs=(
            P(("fsdp", "dp"), None, "tensor"),
            P("tensor"),
            P(("fsdp", "dp"), "tensor"),
            P(("fsdp", "dp"), "tensor"),
        ),
        check_vma=False,
    )
```

```python
import jax
import jax.numpy as jnp
from jax import lax
from jax.experimental import pallas as pl
from jax.experimental.pallas import tpu as pltpu
from jax.sharding import PartitionSpec as P

norm_epsilon = 1e-05
AXES = ("tensor", "fsdp", "dp")
NX, NY, NZ = 4, 4, 8
BF = jnp.bfloat16
F32 = jnp.float32
TOK = 320
BLK = 256
FEATS = 4096
UNITS = 896
EXTRA = 16
IN_A = 160
OUT_A = 128
CUT = 96
FULL = 384
HALF = 64


def _index(x, c, y, z):
    return (((y % NY) // 2) * NZ + z % NZ) * 16 + ((x % NX) * 2 + c % 2) * 2 + y % 2


def _pairs(dx=0, dc=0, dy=0, dz=0, flip=0, turn=False):
    pairs = []
    for x in range(NX):
        for c in range(2):
            way = -1 if turn and c else 1
            for y in range(NY):
                for z in range(NZ):
                    to = (y ^ flip) + way * dy
                    there = _index(x + way * dx, c + dc, to, z + way * dz)
                    pairs.append((_index(x, c, y, z), there))
    return pairs


def move(value, **step):
    return lax.ppermute(value, AXES, _pairs(**step))


def swap_z(blocks):
    lines = [[half * NZ + z for z in range(NZ)] for half in range(2)]
    return lax.all_to_all(
        blocks, "tensor", split_axis=0, concat_axis=0, tiled=True, axis_index_groups=lines
    )


def after(value, *others):
    return lax.optimization_barrier((value, *others))[0]


def add(*terms):
    total = terms[0].astype(F32)
    for term in terms[1:]:
        total = total + term.astype(F32)
    return total


PIECES = 13
CHUNK = 64


def forward_kernel(idx, *refs):
    w, grad, scaled_out, slopes, ready, corr, inverse = refs[PIECES : PIECES + 7]
    acc, square, held, sems, *here = refs[PIECES + 7 : 2 * PIECES + 11]
    piece_sems, scaled, out_sems = refs[2 * PIECES + 11 :]
    line, twin, upper, lower, cross = here[:5]
    pieces_a = ([line], [twin], [upper, lower], [cross])
    pieces_b = here[5:]

    def fetch(k):
        there = pl.ds(pl.multiple_of(idx[k] * BLK, BLK), BLK)
        return pltpu.make_async_copy(w.at[there], held.at[pl.ds(k * BLK, BLK)], sems.at[k])

    def bring(i):
        return pltpu.make_async_copy(refs[i], here[i], piece_sems.at[i])

    def put(group):
        lanes = pl.ds(4 * group * BLK, 4 * BLK)
        return pltpu.make_async_copy(scaled.at[:, lanes], scaled_out.at[:, lanes], out_sems.at[group])

    needed = ((0, 1, 5, 6, 7, 8), (9, 10, 11, 12), (2, 3, 4), ())
    for group in range(4):
        for i in needed[group]:
            bring(i).start()
        for k in range(4 * group, 4 * group + 4):
            fetch(k).start()
    square[...] = jnp.zeros_like(square)
    for group in range(4):
        h, quad = group // 2, group % 2
        for i in needed[group]:
            bring(i).wait()
        for m in range(2):
            j = 2 * h + m
            sums_a, sums_b = [], []
            for q in range(4):
                p = 4 * quad + q
                lanes = pl.ds((4 * group + q) * BLK, BLK)
                at = lax.rem(idx[8 * h + p], NZ)
                head = pieces_a[j][0][at, 0:EXTRA, :].astype(F32)
                gain = head[0:1] + head[1:2]
                row, skip = m * TOK, EXTRA
                for piece in pieces_a[j]:
                    x = piece[at, skip:, :].astype(F32)
                    scaled[pl.ds(row, x.shape[0]), lanes] = (x * gain).astype(BF)
                    sq = x * x
                    sums_a.append((row, sq[:, :128] + sq[:, 128:]))
                    row, skip = row + x.shape[0], 0
                x = pieces_b[p][j].astype(F32)
                scaled[pl.ds(m * TOK + IN_A, TOK - IN_A), lanes] = (x * gain).astype(BF)
                sq = x * x
                sums_b.append(sq[:, :128] + sq[:, 128:])
            for row in sorted({row for row, _ in sums_a}):
                terms = [sq for at, sq in sums_a if at == row]
                square[pl.ds(row, terms[0].shape[0]), :] += sum(terms[1:], terms[0])
            square[pl.ds(m * TOK + IN_A, TOK - IN_A), :] += sum(sums_b[1:], sums_b[0])
        for q in range(4):
            fetch(4 * group + q).wait()
        put(group).start()
        lanes = pl.ds(4 * group * BLK, 4 * BLK)
        product = jnp.dot(scaled[:, lanes], held[lanes, :], preferred_element_type=F32)
        acc[...] = product if group == 0 else acc[...] + product

    first = lax.broadcasted_iota(jnp.int32, (CHUNK, 128), 1) < HALF

    def slope_pair(gate, up, upstream):
        s = 1.0 / (1.0 + jnp.exp(-gate))
        return upstream * up * s * (1.0 + gate * (1.0 - s)), upstream * gate * s

    for chunk in range(2 * TOK // CHUNK):
        rows = pl.ds(chunk * CHUNK, CHUNK)
        mean = jnp.sum(square[rows, :], axis=-1, keepdims=True) / FEATS
        inv = lax.rsqrt(mean + norm_epsilon)
        total = jnp.zeros((CHUNK, 128), F32)
        for tile in range(FULL // 128):
            here, there = pl.ds(tile * 128, 128), pl.ds(FULL + 128 + tile * 128, 128)
            gate, up = acc[rows, here] * inv, acc[rows, there] * inv
            down, lift = slope_pair(gate, up, grad[rows, here].astype(F32))
            slopes[rows, here] = down.astype(BF)
            slopes[rows, there] = lift.astype(BF)
            ready[rows, here] = (down * inv).astype(BF)
            ready[rows, there] = (lift * inv).astype(BF)
            total += down * gate + lift * up
        here = pl.ds(FULL, 128)
        mixed = acc[rows, here] * inv
        turned = pltpu.roll(mixed, HALF, 1)
        gate, up = jnp.where(first, mixed, turned), jnp.where(first, turned, mixed)
        down, lift = slope_pair(gate, up, grad[rows, here].astype(F32))
        both = jnp.where(first, down, lift)
        slopes[rows, here] = both.astype(BF)
        ready[rows, here] = (both * inv).astype(BF)
        total += both * mixed
        corr[rows, :] = jnp.sum(total, axis=-1, keepdims=True) / inv
        inverse[rows, :] = inv
    for group in range(4):
        put(group).wait()


def input_kernel(idx, slopes, w, extra, before, own_a, par_a, out_b, held, sems):
    def fetch(k):
        there = pl.ds(pl.multiple_of(idx[k] * BLK, BLK), BLK)
        return pltpu.make_async_copy(w.at[there], held.at[k], sems.at[k])

    for k in range(16):
        fetch(k).start()
    for k in range(16):
        fetch(k).wait()
        part = lax.dot_general(
            slopes[...], held[k], (((1,), (1,)), ((), ())), preferred_element_type=F32
        ).astype(BF)
        h, p = k // NZ, k % NZ
        at = lax.rem(idx[k], NZ)
        for m, (out_a, slot) in enumerate(((own_a, h), (par_a, idx[16 + h]))):
            out_a[slot, at, :EXTRA, :] = extra[m]
            out_a[slot, at, EXTRA:, :] = part[m * TOK : m * TOK + OUT_A]
            out_b[p, 2 * h + m] = part[m * TOK + OUT_A : (m + 1) * TOK]


def weight_kernel(idx, x0, x1, x2, x3, ready, *refs):
    got, out = refs[:-1], refs[-1]
    for q, x in enumerate((x0, x1, x2, x3)):
        part = lax.dot_general(
            x[...], ready[...], (((0,), (0,)), ((), ())), preferred_element_type=F32
        )
        out[q] = (part + got[0][q].astype(F32) if got else part).astype(BF)


MIB = 1024 * 1024


def _params():
    return pltpu.CompilerParams(dimension_semantics=("arbitrary",), vmem_limit_bytes=22 * MIB)


def _cost(flops, moved, exps=0):
    return pl.CostEstimate(flops=flops, bytes_accessed=moved, transcendentals=exps)


def _still(*shape):
    return pl.BlockSpec(shape, lambda *_: (0,) * len(shape))


def forward(idx, pieces, weights, grad):
    smem = pl.BlockSpec(memory_space=pltpu.SMEM)
    vmem = pl.BlockSpec(memory_space=pltpu.VMEM)
    hbm = pl.BlockSpec(memory_space=pltpu.HBM)
    return pl.pallas_call(
        forward_kernel,
        in_specs=[smem, *[hbm] * (PIECES + 1), vmem],
        out_specs=[pl.BlockSpec(memory_space=pl.ANY), *[vmem] * 4],
        scratch_shapes=[
            pltpu.VMEM((2 * TOK, UNITS), F32),
            pltpu.VMEM((2 * TOK, 128), F32),
            pltpu.VMEM((FEATS, UNITS), BF),
            pltpu.SemaphoreType.DMA((16,)),
            *[pltpu.VMEM(piece.shape, BF) for piece in pieces],
            pltpu.SemaphoreType.DMA((PIECES,)),
            pltpu.VMEM((2 * TOK, FEATS), BF),
            pltpu.SemaphoreType.DMA((4,)),
        ],
        out_shape=[
            jax.ShapeDtypeStruct((2 * TOK, FEATS), BF),
            jax.ShapeDtypeStruct((2 * TOK, UNITS), BF),
            jax.ShapeDtypeStruct((2 * TOK, UNITS), BF),
            jax.ShapeDtypeStruct((2 * TOK, 1), F32),
            jax.ShapeDtypeStruct((2 * TOK, 1), F32),
        ],
        compiler_params=pltpu.CompilerParams(vmem_limit_bytes=52 * MIB),
        cost_estimate=_cost(2 * 640 * FEATS * UNITS, 14 << 20, 640 * 512),
        name="forward_slopes",
    )(idx, *pieces, weights, grad)


def input_parts(idx, slopes, weights, extra, before):
    vmem = pl.BlockSpec(memory_space=pltpu.VMEM)
    return pl.pallas_call(
        input_kernel,
        in_specs=[
            pl.BlockSpec(memory_space=pltpu.SMEM),
            vmem,
            pl.BlockSpec(memory_space=pltpu.HBM),
            vmem,
            pl.BlockSpec(memory_space=pl.ANY),
        ],
        out_specs=[vmem] * 3,
        scratch_shapes=[pltpu.VMEM((16, BLK, UNITS), BF), pltpu.SemaphoreType.DMA((16,))],
        out_shape=[
            *[jax.ShapeDtypeStruct((2, NZ, EXTRA + OUT_A, BLK), BF)] * 2,
            jax.ShapeDtypeStruct((NZ, 4, TOK - OUT_A, BLK), BF),
        ],
        compiler_params=pltpu.CompilerParams(vmem_limit_bytes=40 * MIB),
        cost_estimate=_cost(2 * 640 * FEATS * UNITS, 14 << 20),
        name="input_parts",
    )(idx, slopes, weights, extra, before)


def weight_parts(idx, scaled, ready, *got):
    blocks = pl.BlockSpec((4, BLK, UNITS), lambda s, i: (s, 0, 0))
    return pl.pallas_call(
        weight_kernel,
        grid_spec=pltpu.PrefetchScalarGridSpec(
            num_scalar_prefetch=1,
            grid=(2,),
            in_specs=[
                *[
                    pl.BlockSpec((2 * TOK, BLK), lambda s, i, q=q: (0, i[4 * s + q]))
                    for q in range(4)
                ],
                _still(2 * TOK, UNITS),
                *[blocks] * len(got),
            ],
            out_specs=blocks,
        ),
        out_shape=jax.ShapeDtypeStruct((8, BLK, UNITS), BF),
        compiler_params=_params(),
        cost_estimate=_cost(640 * FEATS * UNITS, 7 << 20),
        name="weight_parts",
    )(idx, *[scaled] * 4, ready, *got)


def gather_plane(shard, gain, pair):
    high = gain.astype(BF)
    low = (gain - high.astype(F32)).astype(BF)
    head = jnp.concatenate([high[None], low[None], jnp.zeros((EXTRA - 2, BLK), BF)], axis=0)
    part_a = jnp.concatenate([head, shard[:IN_A]], axis=0)
    part_b = shard[IN_A:]
    rows = {0: jnp.stack([part_b] + [move(part_b, flip=j) for j in (1, 2, 3)])}
    line = swap_z(jnp.broadcast_to(part_a, (NZ, *part_a.shape)))
    rows[1], rows[7] = move(rows[0], dz=-1, turn=True), move(rows[0], dz=1, turn=True)
    line = after(line, pair)
    twin, cross = move(line, flip=1), move(line, flip=3)
    rows[1], rows[7] = after((rows[1], rows[7]), line)
    for p in (2, 3):
        rows[p] = move(rows[p - 1], dz=-1, turn=True)
        rows[8 - p] = move(rows[(9 - p) % 8], dz=1, turn=True)
    rows[4] = move(rows[3], dz=-1, turn=True)
    upper, lower = move(twin[:, :CUT], flip=3), move(cross[:, CUT:], flip=1)
    return [line, twin, upper, lower, cross] + [rows[p] for p in range(NZ)]


def pick(first, second, d):
    return jnp.where(d == 0, first, second)


def mine(left, right, d):
    rest = FULL + 2 * HALF
    return jnp.concatenate(
        [
            pick(left[:, :FULL], left[:, rest:], d),
            pick(left[:, FULL : FULL + HALF], left[:, FULL + HALF : rest], d),
            pick(right[:, FULL : FULL + HALF], right[:, FULL + HALF : rest], d),
            pick(right[:, :FULL], right[:, rest:], d),
        ],
        axis=1,
    )


def tables():
    tensor, fsdp, d = (lax.axis_index(axis).astype(jnp.int32) for axis in AXES)
    y_hi, z = tensor // NZ, tensor % NZ
    x, c = fsdp // 2, fsdp % 2
    k = jnp.arange(16, dtype=jnp.int32)
    block = ((y_hi + k // 8) % 2) * NZ + (z + (1 - 2 * c) * (k % 8)) % NZ
    order = jnp.concatenate([block, jnp.stack([d ^ c, 1 - (d ^ c)])])

    def of_core(core):
        s = jnp.arange(8, dtype=jnp.int32)
        to = x + (1 - 2 * core) * (s // 2)
        g = ((to % NX) * 2 + core) * 2 + s % 2
        h, p = (g // NZ - y_hi) % 2, ((1 - 2 * c) * (g % NZ - z)) % NZ
        return h * NZ + p

    return block, order, of_core(1 - c), of_core(c), d


def body(inputs, norm_gain, gate_weight, up_weight, hidden_grad):
    block, order, other_core, this_core, d = tables()
    weights = lax.all_gather(mine(gate_weight, up_weight, d), "fsdp", axis=0, tiled=True)

    grad = hidden_grad[0]
    keep = mine(grad, grad, d)[:, : FULL + 128]
    give = mine(grad, grad, 1 - d)[:, : FULL + 128]
    received = move(give, flip=1)
    grads = jnp.concatenate([keep, received], axis=0)

    local_x = inputs[0]
    pieces = gather_plane(local_x, norm_gain, received)
    scaled, slopes, ready, corr, inverse = forward(block, pieces, weights, grads)

    rows = jnp.pad(corr.reshape(2, TOK) / FEATS, ((0, 0), (0, 512 - TOK))).reshape(2, 2, BLK)
    extra = jnp.pad(rows, ((0, 0), (0, EXTRA - 2), (0, 0))).astype(BF)
    theirs = weight_parts(other_core, scaled, ready)
    got = move(theirs, dc=1)
    own_a, par_a, part_b = input_parts(order, slopes, weights, extra, theirs)

    ring_y = move(par_a[1], dy=1, turn=True)
    up = move(part_b[4], dz=1, turn=True)
    ours = weight_parts(this_core, scaled, after(ready, part_b), got)
    parts = [ours[2 * k : 2 * k + 2] for k in range(NX)]

    ring_y, up = after((ring_y, up), ours)
    ring_y = add(own_a[1], ring_y).astype(BF)
    up, down = add(part_b[3], up).astype(BF), part_b[5]
    ring_y, up, down = after((ring_y, up, down))
    ring_y = move(ring_y, dy=1, turn=True)
    up, down = move(up, dz=1, turn=True), move(down, dz=-1, turn=True)
    x_next = move(parts[1], dx=1, turn=True)

    ring_y = add(par_a[0], ring_y).astype(BF)
    up, down = add(part_b[2], up).astype(BF), add(part_b[6], down).astype(BF)
    ring_y, up, down = after((ring_y, up, down))
    ring_y = move(ring_y, dy=1, turn=True)
    up, down = move(up, dz=1, turn=True), move(down, dz=-1, turn=True)

    line = add(own_a[0], ring_y).astype(BF)
    up, down = add(part_b[1], up).astype(BF), add(part_b[7], down).astype(BF)
    line, up, down, far_x, last_x = after((line, up, down, parts[2], parts[3]), x_next)
    up, down = move(up, dz=1, turn=True), move(down, dz=-1, turn=True)
    line = swap_z(line)
    x_across, x_back = move(far_x, dx=2), move(last_x, dx=-1, turn=True)

    column = add(part_b[0], up, down)
    sent = column.astype(BF)
    sum_b = add(column[0], *[move(sent[j], flip=j) for j in (1, 2, 3)])
    sum_a = jnp.sum(line.astype(F32), axis=0)
    x_across, x_back = after((x_across, x_back), sum_b)
    rows = add(parts[0], x_next, x_across, x_back)
    rows_0, rows_1 = rows[0], rows[1]
    keep = pick(rows_0, rows_1, d).astype(BF)
    got = move(pick(rows_1, rows_0, d).astype(BF), flip=1)

    def whole(start, shared):
        left, right = pick(keep, got, d), pick(got, keep, d)
        return jnp.concatenate(
            [
                left[:, start : start + FULL],
                left[:, shared : shared + HALF],
                right[:, shared : shared + HALF],
                right[:, start : start + FULL],
            ],
            axis=1,
        )

    gate_grad = whole(0, FULL)
    up_grad = whole(FULL + 128, FULL + HALF)

    normed_grad = jnp.concatenate([sum_a[EXTRA:], sum_b], axis=0)
    correction = sum_a[:2].reshape(512)[:TOK][:, None]
    inv = inverse[:TOK]
    x = local_x.astype(F32)
    input_grad = inv * (normed_grad * norm_gain) - x * inv * inv * inv * correction
    gain_part = jnp.sum(normed_grad * x * inv, axis=0).reshape(2, 128)
    gain_part = gain_part + move(gain_part, dc=1)
    gain_part = (
        gain_part + move(gain_part, dx=1) + move(gain_part, dx=-1) + move(gain_part, dx=2)
    )
    gain_grad = (gain_part + move(gain_part, flip=1)).reshape(BLK)
    return input_grad.astype(BF)[None], gain_grad, gate_grad, up_grad


def solution(mesh):
    placed = (
        P(("fsdp", "dp"), None, "tensor"),
        P("tensor"),
        P("fsdp", "tensor"),
        P("fsdp", "tensor"),
        P(("fsdp", "dp"), None, "tensor"),
    )
    return jax.shard_map(
        body,
        mesh=mesh,
        in_specs=placed,
        out_specs=(
            P(("fsdp", "dp"), None, "tensor"),
            P("tensor"),
            P(("fsdp", "dp"), "tensor"),
            P(("fsdp", "dp"), "tensor"),
        ),
        check_vma=False,
    )
```

```python
import jax
import jax.numpy as jnp
from jax import lax
from jax.experimental import pallas as pl
from jax.experimental.pallas import tpu as pltpu
from jax.sharding import PartitionSpec as P

norm_epsilon = 1e-05
AXES = ("tensor", "fsdp", "dp")
NX, NY, NZ = 4, 4, 8
BF = jnp.bfloat16
F32 = jnp.float32
TOK = 320
BLK = 256
FEATS = 4096
UNITS = 896
EXTRA = 16
IN_A = 160
OUT_A = 128
CUT = 96
FULL = 384
HALF = 64


def _index(x, c, y, z):
    return (((y % NY) // 2) * NZ + z % NZ) * 16 + ((x % NX) * 2 + c % 2) * 2 + y % 2


def _pairs(dx=0, dc=0, dy=0, dz=0, flip=0, turn=False):
    pairs = []
    for x in range(NX):
        for c in range(2):
            way = -1 if turn and c else 1
            for y in range(NY):
                for z in range(NZ):
                    to = (y ^ flip) + way * dy
                    there = _index(x + way * dx, c + dc, to, z + way * dz)
                    pairs.append((_index(x, c, y, z), there))
    return pairs


def move(value, **step):
    return lax.ppermute(value, AXES, _pairs(**step))


def swap_z(blocks):
    lines = [[half * NZ + z for z in range(NZ)] for half in range(2)]
    return lax.all_to_all(
        blocks, "tensor", split_axis=0, concat_axis=0, tiled=True, axis_index_groups=lines
    )


def after(value, *others):
    return lax.optimization_barrier((value, *others))[0]


def add(*terms):
    total = terms[0].astype(F32)
    for term in terms[1:]:
        total = total + term.astype(F32)
    return total


PIECES = 13
CHUNK = 64


def forward_kernel(idx, *refs):
    w, grad, scaled_out, slopes, ready, corr, inverse = refs[PIECES : PIECES + 7]
    acc, square, held, sems, *here = refs[PIECES + 7 : 2 * PIECES + 11]
    piece_sems, scaled, out_sems = refs[2 * PIECES + 11 :]
    line, twin, upper, lower, cross = here[:5]
    pieces_a = ([line], [twin], [upper, lower], [cross])
    pieces_b = here[5:]

    def fetch(k):
        there = pl.ds(pl.multiple_of(idx[k] * BLK, BLK), BLK)
        return pltpu.make_async_copy(w.at[there], held.at[pl.ds(k * BLK, BLK)], sems.at[k])

    def bring(i):
        return pltpu.make_async_copy(refs[i], here[i], piece_sems.at[i])

    def put(group):
        lanes = pl.ds(4 * group * BLK, 4 * BLK)
        return pltpu.make_async_copy(scaled.at[:, lanes], scaled_out.at[:, lanes], out_sems.at[group])

    needed = ((0, 1, 5, 6, 7, 8), (9, 10, 11, 12), (2, 3, 4), ())
    for group in range(4):
        for i in needed[group]:
            bring(i).start()
        for k in range(4 * group, 4 * group + 4):
            fetch(k).start()
    square[...] = jnp.zeros_like(square)
    for group in range(4):
        h, quad = group // 2, group % 2
        for i in needed[group]:
            bring(i).wait()
        for m in range(2):
            j = 2 * h + m
            sums_a, sums_b = [], []
            for q in range(4):
                p = 4 * quad + q
                lanes = pl.ds((4 * group + q) * BLK, BLK)
                at = lax.rem(idx[8 * h + p], NZ)
                head = pieces_a[j][0][at, 0:EXTRA, :].astype(F32)
                gain = head[0:1] + head[1:2]
                row, skip = m * TOK, EXTRA
                for piece in pieces_a[j]:
                    x = piece[at, skip:, :].astype(F32)
                    scaled[pl.ds(row, x.shape[0]), lanes] = (x * gain).astype(BF)
                    sq = x * x
                    sums_a.append((row, sq[:, :128] + sq[:, 128:]))
                    row, skip = row + x.shape[0], 0
                x = pieces_b[p][j].astype(F32)
                scaled[pl.ds(m * TOK + IN_A, TOK - IN_A), lanes] = (x * gain).astype(BF)
                sq = x * x
                sums_b.append(sq[:, :128] + sq[:, 128:])
            for row in sorted({row for row, _ in sums_a}):
                terms = [sq for at, sq in sums_a if at == row]
                square[pl.ds(row, terms[0].shape[0]), :] += sum(terms[1:], terms[0])
            square[pl.ds(m * TOK + IN_A, TOK - IN_A), :] += sum(sums_b[1:], sums_b[0])
        for q in range(4):
            fetch(4 * group + q).wait()
        put(group).start()
        lanes = pl.ds(4 * group * BLK, 4 * BLK)
        product = jnp.dot(scaled[:, lanes], held[lanes, :], preferred_element_type=F32)
        acc[...] = product if group == 0 else acc[...] + product

    first = lax.broadcasted_iota(jnp.int32, (CHUNK, 128), 1) < HALF

    def slope_pair(gate, up, upstream):
        s = 1.0 / (1.0 + jnp.exp(-gate))
        return upstream * up * s * (1.0 + gate * (1.0 - s)), upstream * gate * s

    for chunk in range(2 * TOK // CHUNK):
        rows = pl.ds(chunk * CHUNK, CHUNK)
        mean = jnp.sum(square[rows, :], axis=-1, keepdims=True) / FEATS
        inv = lax.rsqrt(mean + norm_epsilon)
        total = jnp.zeros((CHUNK, 128), F32)
        for tile in range(FULL // 128):
            here, there = pl.ds(tile * 128, 128), pl.ds(FULL + 128 + tile * 128, 128)
            gate, up = acc[rows, here] * inv, acc[rows, there] * inv
            down, lift = slope_pair(gate, up, grad[rows, here].astype(F32))
            slopes[rows, here] = down.astype(BF)
            slopes[rows, there] = lift.astype(BF)
            ready[rows, here] = (down * inv).astype(BF)
            ready[rows, there] = (lift * inv).astype(BF)
            total += down * gate + lift * up
        here = pl.ds(FULL, 128)
        mixed = acc[rows, here] * inv
        turned = pltpu.roll(mixed, HALF, 1)
        gate, up = jnp.where(first, mixed, turned), jnp.where(first, turned, mixed)
        down, lift = slope_pair(gate, up, grad[rows, here].astype(F32))
        both = jnp.where(first, down, lift)
        slopes[rows, here] = both.astype(BF)
        ready[rows, here] = (both * inv).astype(BF)
        total += both * mixed
        corr[rows, :] = jnp.sum(total, axis=-1, keepdims=True) / inv
        inverse[rows, :] = inv
    for group in range(4):
        put(group).wait()


def input_kernel(idx, slopes, w0, w1, w2, w3, extra, before, own_a, par_a, out_b):
    step = pl.program_id(0)
    for q, w in enumerate((w0, w1, w2, w3)):
        part = lax.dot_general(
            slopes[...], w[...], (((1,), (1,)), ((), ())), preferred_element_type=F32
        ).astype(BF)
        at = lax.rem(idx[4 * step + q], NZ)
        for m, out_a in enumerate((own_a, par_a)):
            out_a[0, at, :EXTRA, :] = extra[m]
            out_a[0, at, EXTRA:, :] = part[m * TOK : m * TOK + OUT_A]
            out_b[q, m] = part[m * TOK + OUT_A : (m + 1) * TOK]


def weight_kernel(idx, x0, x1, x2, x3, ready, *refs):
    got, out = refs[:-1], refs[-1]
    for q, x in enumerate((x0, x1, x2, x3)):
        part = lax.dot_general(
            x[...], ready[...], (((0,), (0,)), ((), ())), preferred_element_type=F32
        )
        out[q] = (part + got[0][q].astype(F32) if got else part).astype(BF)


MIB = 1024 * 1024


def _params():
    return pltpu.CompilerParams(dimension_semantics=("arbitrary",), vmem_limit_bytes=56 * MIB)


def _cost(flops, moved, exps=0):
    return pl.CostEstimate(flops=flops, bytes_accessed=moved, transcendentals=exps)


def _still(*shape):
    return pl.BlockSpec(shape, lambda *_: (0,) * len(shape))


def forward(idx, pieces, weights, grad):
    smem = pl.BlockSpec(memory_space=pltpu.SMEM)
    vmem = pl.BlockSpec(memory_space=pltpu.VMEM)
    hbm = pl.BlockSpec(memory_space=pltpu.HBM)
    return pl.pallas_call(
        forward_kernel,
        in_specs=[smem, *[hbm] * (PIECES + 1), vmem],
        out_specs=[pl.BlockSpec(memory_space=pl.ANY), *[vmem] * 4],
        scratch_shapes=[
            pltpu.VMEM((2 * TOK, UNITS), F32),
            pltpu.VMEM((2 * TOK, 128), F32),
            pltpu.VMEM((FEATS, UNITS), BF),
            pltpu.SemaphoreType.DMA((16,)),
            *[pltpu.VMEM(piece.shape, BF) for piece in pieces],
            pltpu.SemaphoreType.DMA((PIECES,)),
            pltpu.VMEM((2 * TOK, FEATS), BF),
            pltpu.SemaphoreType.DMA((4,)),
        ],
        out_shape=[
            jax.ShapeDtypeStruct((2 * TOK, FEATS), BF),
            jax.ShapeDtypeStruct((2 * TOK, UNITS), BF),
            jax.ShapeDtypeStruct((2 * TOK, UNITS), BF),
            jax.ShapeDtypeStruct((2 * TOK, 1), F32),
            jax.ShapeDtypeStruct((2 * TOK, 1), F32),
        ],
        compiler_params=pltpu.CompilerParams(vmem_limit_bytes=52 * MIB),
        cost_estimate=_cost(2 * 640 * FEATS * UNITS, 14 << 20, 640 * 512),
        name="forward_slopes",
    )(idx, *pieces, weights, grad)


def input_parts(idx, slopes, weights, extra, before):
    return pl.pallas_call(
        input_kernel,
        grid_spec=pltpu.PrefetchScalarGridSpec(
            num_scalar_prefetch=1,
            grid=(4,),
            in_specs=[
                _still(2 * TOK, UNITS),
                *[
                    pl.BlockSpec((BLK, UNITS), lambda k, i, q=q: (i[4 * k + q], 0))
                    for q in range(4)
                ],
                _still(2, EXTRA, BLK),
                pl.BlockSpec(memory_space=pl.ANY),
            ],
            out_specs=[
                pl.BlockSpec((1, NZ, EXTRA + OUT_A, BLK), lambda k, i: (k // 2, 0, 0, 0)),
                pl.BlockSpec((1, NZ, EXTRA + OUT_A, BLK), lambda k, i: (i[16 + k // 2], 0, 0, 0)),
                pl.BlockSpec((4, 2, TOK - OUT_A, BLK), lambda k, i: (k % 2, k // 2, 0, 0)),
            ],
        ),
        out_shape=[
            *[jax.ShapeDtypeStruct((2, NZ, EXTRA + OUT_A, BLK), BF)] * 2,
            jax.ShapeDtypeStruct((NZ, 4, TOK - OUT_A, BLK), BF),
        ],
        compiler_params=_params(),
        cost_estimate=_cost(2 * 640 * FEATS * UNITS, 14 << 20),
        name="input_parts",
    )(idx, slopes, *[weights] * 4, extra, before)


def weight_parts(idx, scaled, ready, *got):
    blocks = pl.BlockSpec((4, BLK, UNITS), lambda s, i: (s, 0, 0))
    return pl.pallas_call(
        weight_kernel,
        grid_spec=pltpu.PrefetchScalarGridSpec(
            num_scalar_prefetch=1,
            grid=(2,),
            in_specs=[
                *[
                    pl.BlockSpec((2 * TOK, BLK), lambda s, i, q=q: (0, i[4 * s + q]))
                    for q in range(4)
                ],
                _still(2 * TOK, UNITS),
                *[blocks] * len(got),
            ],
            out_specs=blocks,
        ),
        out_shape=jax.ShapeDtypeStruct((8, BLK, UNITS), BF),
        compiler_params=_params(),
        cost_estimate=_cost(640 * FEATS * UNITS, 7 << 20),
        name="weight_parts",
    )(idx, *[scaled] * 4, ready, *got)


def gather_plane(shard, gain, pair):
    high = gain.astype(BF)
    low = (gain - high.astype(F32)).astype(BF)
    head = jnp.concatenate([high[None], low[None], jnp.zeros((EXTRA - 2, BLK), BF)], axis=0)
    part_a = jnp.concatenate([head, shard[:IN_A]], axis=0)
    part_b = shard[IN_A:]
    rows = {0: jnp.stack([part_b] + [move(part_b, flip=j) for j in (1, 2, 3)])}
    line = swap_z(jnp.broadcast_to(part_a, (NZ, *part_a.shape)))
    rows[1], rows[7] = move(rows[0], dz=-1, turn=True), move(rows[0], dz=1, turn=True)
    line = after(line, pair)
    twin, cross = move(line, flip=1), move(line, flip=3)
    rows[1], rows[7] = after((rows[1], rows[7]), line)
    for p in (2, 3):
        rows[p] = move(rows[p - 1], dz=-1, turn=True)
        rows[8 - p] = move(rows[(9 - p) % 8], dz=1, turn=True)
    rows[4] = move(rows[3], dz=-1, turn=True)
    upper, lower = move(twin[:, :CUT], flip=3), move(cross[:, CUT:], flip=1)
    return [line, twin, upper, lower, cross] + [rows[p] for p in range(NZ)]


def pick(first, second, d):
    return jnp.where(d == 0, first, second)


def mine(left, right, d):
    rest = FULL + 2 * HALF
    return jnp.concatenate(
        [
            pick(left[:, :FULL], left[:, rest:], d),
            pick(left[:, FULL : FULL + HALF], left[:, FULL + HALF : rest], d),
            pick(right[:, FULL : FULL + HALF], right[:, FULL + HALF : rest], d),
            pick(right[:, :FULL], right[:, rest:], d),
        ],
        axis=1,
    )


def tables():
    tensor, fsdp, d = (lax.axis_index(axis).astype(jnp.int32) for axis in AXES)
    y_hi, z = tensor // NZ, tensor % NZ
    x, c = fsdp // 2, fsdp % 2
    k = jnp.arange(16, dtype=jnp.int32)
    block = ((y_hi + k // 8) % 2) * NZ + (z + (1 - 2 * c) * (k % 8)) % NZ
    order = jnp.concatenate([block, jnp.stack([d ^ c, 1 - (d ^ c)])])

    def of_core(core):
        s = jnp.arange(8, dtype=jnp.int32)
        to = x + (1 - 2 * core) * (s // 2)
        g = ((to % NX) * 2 + core) * 2 + s % 2
        h, p = (g // NZ - y_hi) % 2, ((1 - 2 * c) * (g % NZ - z)) % NZ
        return h * NZ + p

    return block, order, of_core(1 - c), of_core(c), d


def body(inputs, norm_gain, gate_weight, up_weight, hidden_grad):
    block, order, other_core, this_core, d = tables()
    weights = lax.all_gather(mine(gate_weight, up_weight, d), "fsdp", axis=0, tiled=True)

    grad = hidden_grad[0]
    keep = mine(grad, grad, d)[:, : FULL + 128]
    give = mine(grad, grad, 1 - d)[:, : FULL + 128]
    received = move(give, flip=1)
    grads = jnp.concatenate([keep, received], axis=0)

    local_x = inputs[0]
    pieces = gather_plane(local_x, norm_gain, received)
    scaled, slopes, ready, corr, inverse = forward(block, pieces, weights, grads)

    rows = jnp.pad(corr.reshape(2, TOK) / FEATS, ((0, 0), (0, 512 - TOK))).reshape(2, 2, BLK)
    extra = jnp.pad(rows, ((0, 0), (0, EXTRA - 2), (0, 0))).astype(BF)
    own_a, par_a, part_b = input_parts(order, slopes, weights, extra, ready)
    ring_y = move(par_a[1], dy=1, turn=True)
    up = move(part_b[4], dz=1, turn=True)
    theirs = weight_parts(other_core, scaled, after(ready, part_b))

    ring_y, up = after((ring_y, up), theirs)
    got = move(after(theirs, ring_y, up), dc=1)
    ring_y = add(own_a[1], ring_y).astype(BF)
    up, down = add(part_b[3], up).astype(BF), part_b[5]
    ring_y, up, down = after((ring_y, up, down))
    ours = weight_parts(this_core, scaled, after(ready, ring_y, up), got)
    parts = [ours[2 * k : 2 * k + 2] for k in range(NX)]
    ring_y = move(ring_y, dy=1, turn=True)
    up, down = move(up, dz=1, turn=True), move(down, dz=-1, turn=True)

    ring_y, up, down = after((ring_y, up, down), ours)
    ring_y = add(par_a[0], ring_y).astype(BF)
    up, down = add(part_b[2], up).astype(BF), add(part_b[6], down).astype(BF)
    ring_y, up, down = after((ring_y, up, down))
    x_next = move(parts[1], dx=1, turn=True)
    ring_y = move(ring_y, dy=1, turn=True)
    up, down = move(up, dz=1, turn=True), move(down, dz=-1, turn=True)

    line = add(own_a[0], ring_y).astype(BF)
    up, down = add(part_b[1], up).astype(BF), add(part_b[7], down).astype(BF)
    line, up, down, far_x = after((line, up, down, parts[2]), x_next)
    up, down = move(up, dz=1, turn=True), move(down, dz=-1, turn=True)
    line = swap_z(line)
    x_across = move(far_x, dx=2)

    column, last_x = add(part_b[0], up, down), parts[3]
    column, x_across, last_x = after((column, x_across, last_x))
    x_back = move(last_x, dx=-1, turn=True)
    sent = column.astype(BF)
    sum_b = add(column[0], *[move(sent[j], flip=j) for j in (1, 2, 3)])
    sum_a = jnp.sum(line.astype(F32), axis=0)
    x_back = after(x_back, sum_b)
    rows = add(parts[0], x_next, x_across, x_back)
    rows_0, rows_1 = rows[0], rows[1]
    keep = pick(rows_0, rows_1, d).astype(BF)
    got = move(pick(rows_1, rows_0, d).astype(BF), flip=1)

    def whole(start, shared):
        left, right = pick(keep, got, d), pick(got, keep, d)
        return jnp.concatenate(
            [
                left[:, start : start + FULL],
                left[:, shared : shared + HALF],
                right[:, shared : shared + HALF],
                right[:, start : start + FULL],
            ],
            axis=1,
        )

    gate_grad = whole(0, FULL)
    up_grad = whole(FULL + 128, FULL + HALF)

    normed_grad = jnp.concatenate([sum_a[EXTRA:], sum_b], axis=0)
    correction = sum_a[:2].reshape(512)[:TOK][:, None]
    inv = inverse[:TOK]
    x = local_x.astype(F32)
    input_grad = inv * (normed_grad * norm_gain) - x * inv * inv * inv * correction
    gain_part = jnp.sum(normed_grad * x * inv, axis=0).reshape(2, 128)
    gain_part = gain_part + move(gain_part, dc=1)
    gain_part = (
        gain_part + move(gain_part, dx=1) + move(gain_part, dx=-1) + move(gain_part, dx=2)
    )
    gain_grad = (gain_part + move(gain_part, flip=1)).reshape(BLK)
    return input_grad.astype(BF)[None], gain_grad, gate_grad, up_grad


def solution(mesh):
    placed = (
        P(("fsdp", "dp"), None, "tensor"),
        P("tensor"),
        P("fsdp", "tensor"),
        P("fsdp", "tensor"),
        P(("fsdp", "dp"), None, "tensor"),
    )
    return jax.shard_map(
        body,
        mesh=mesh,
        in_specs=placed,
        out_specs=(
            P(("fsdp", "dp"), None, "tensor"),
            P("tensor"),
            P(("fsdp", "dp"), "tensor"),
            P(("fsdp", "dp"), "tensor"),
        ),
        check_vma=False,
    )
```

```python
import jax
import jax.numpy as jnp
from jax import lax
from jax.experimental import pallas as pl
from jax.experimental.pallas import tpu as pltpu
from jax.sharding import PartitionSpec as P

norm_epsilon = 1e-05
AXES = ("tensor", "fsdp", "dp")
NX, NY, NZ = 4, 4, 8
BF = jnp.bfloat16
F32 = jnp.float32
TOK = 320
BLK = 256
FEATS = 4096
UNITS = 896
EXTRA = 16
IN_A = 160
OUT_A = 128
CUT = 96
FULL = 384
HALF = 64


def _index(x, c, y, z):
    return (((y % NY) // 2) * NZ + z % NZ) * 16 + ((x % NX) * 2 + c % 2) * 2 + y % 2


def _pairs(dx=0, dc=0, dy=0, dz=0, flip=0, turn=False):
    pairs = []
    for x in range(NX):
        for c in range(2):
            way = -1 if turn and c else 1
            for y in range(NY):
                for z in range(NZ):
                    to = (y ^ flip) + way * dy
                    there = _index(x + way * dx, c + dc, to, z + way * dz)
                    pairs.append((_index(x, c, y, z), there))
    return pairs


def move(value, **step):
    return lax.ppermute(value, AXES, _pairs(**step))


def swap_z(blocks):
    lines = [[half * NZ + z for z in range(NZ)] for half in range(2)]
    return lax.all_to_all(
        blocks, "tensor", split_axis=0, concat_axis=0, tiled=True, axis_index_groups=lines
    )


def after(value, *others):
    return lax.optimization_barrier((value, *others))[0]


def add(*terms):
    total = terms[0].astype(F32)
    for term in terms[1:]:
        total = total + term.astype(F32)
    return total


PIECES = 13
CHUNK = 64


def forward_kernel(idx, *refs):
    w, grad, scaled_out, slopes, ready, corr, inverse = refs[PIECES : PIECES + 7]
    acc, square, held, sems, *here = refs[PIECES + 7 : 2 * PIECES + 11]
    piece_sems, scaled, out_sems = refs[2 * PIECES + 11 :]
    line, twin, upper, lower, cross = here[:5]
    pieces_a = ([line], [twin], [upper, lower], [cross])
    pieces_b = here[5:]

    def fetch(k):
        there = pl.ds(pl.multiple_of(idx[k] * BLK, BLK), BLK)
        return pltpu.make_async_copy(w.at[there], held.at[pl.ds(k * BLK, BLK)], sems.at[k])

    def bring(i):
        return pltpu.make_async_copy(refs[i], here[i], piece_sems.at[i])

    def put(group):
        lanes = pl.ds(4 * group * BLK, 4 * BLK)
        return pltpu.make_async_copy(scaled.at[:, lanes], scaled_out.at[:, lanes], out_sems.at[group])

    needed = ((0, 1, 5, 6, 7, 8), (9, 10, 11, 12), (2, 3, 4), ())
    for group in range(4):
        for i in needed[group]:
            bring(i).start()
        for k in range(4 * group, 4 * group + 4):
            fetch(k).start()
    square[...] = jnp.zeros_like(square)
    for group in range(4):
        h, quad = group // 2, group % 2
        for i in needed[group]:
            bring(i).wait()
        for m in range(2):
            j = 2 * h + m
            sums_a, sums_b = [], []
            for q in range(4):
                p = 4 * quad + q
                lanes = pl.ds((4 * group + q) * BLK, BLK)
                at = lax.rem(idx[8 * h + p], NZ)
                head = pieces_a[j][0][at, 0:EXTRA, :].astype(F32)
                gain = head[0:1] + head[1:2]
                row, skip = m * TOK, EXTRA
                for piece in pieces_a[j]:
                    x = piece[at, skip:, :].astype(F32)
                    scaled[pl.ds(row, x.shape[0]), lanes] = (x * gain).astype(BF)
                    sq = x * x
                    sums_a.append((row, sq[:, :128] + sq[:, 128:]))
                    row, skip = row + x.shape[0], 0
                x = pieces_b[p][j].astype(F32)
                scaled[pl.ds(m * TOK + IN_A, TOK - IN_A), lanes] = (x * gain).astype(BF)
                sq = x * x
                sums_b.append(sq[:, :128] + sq[:, 128:])
            for row in sorted({row for row, _ in sums_a}):
                terms = [sq for at, sq in sums_a if at == row]
                square[pl.ds(row, terms[0].shape[0]), :] += sum(terms[1:], terms[0])
            square[pl.ds(m * TOK + IN_A, TOK - IN_A), :] += sum(sums_b[1:], sums_b[0])
        for q in range(4):
            fetch(4 * group + q).wait()
        put(group).start()
        lanes = pl.ds(4 * group * BLK, 4 * BLK)
        product = jnp.dot(scaled[:, lanes], held[lanes, :], preferred_element_type=F32)
        acc[...] = product if group == 0 else acc[...] + product

    first = lax.broadcasted_iota(jnp.int32, (CHUNK, 128), 1) < HALF

    def slope_pair(gate, up, upstream):
        s = 1.0 / (1.0 + jnp.exp(-gate))
        return upstream * up * s * (1.0 + gate * (1.0 - s)), upstream * gate * s

    for chunk in range(2 * TOK // CHUNK):
        rows = pl.ds(chunk * CHUNK, CHUNK)
        mean = jnp.sum(square[rows, :], axis=-1, keepdims=True) / FEATS
        inv = lax.rsqrt(mean + norm_epsilon)
        total = jnp.zeros((CHUNK, 128), F32)
        for tile in range(FULL // 128):
            here, there = pl.ds(tile * 128, 128), pl.ds(FULL + 128 + tile * 128, 128)
            gate, up = acc[rows, here] * inv, acc[rows, there] * inv
            down, lift = slope_pair(gate, up, grad[rows, here].astype(F32))
            slopes[rows, here] = down.astype(BF)
            slopes[rows, there] = lift.astype(BF)
            ready[rows, here] = (down * inv).astype(BF)
            ready[rows, there] = (lift * inv).astype(BF)
            total += down * gate + lift * up
        here = pl.ds(FULL, 128)
        mixed = acc[rows, here] * inv
        turned = pltpu.roll(mixed, HALF, 1)
        gate, up = jnp.where(first, mixed, turned), jnp.where(first, turned, mixed)
        down, lift = slope_pair(gate, up, grad[rows, here].astype(F32))
        both = jnp.where(first, down, lift)
        slopes[rows, here] = both.astype(BF)
        ready[rows, here] = (both * inv).astype(BF)
        total += both * mixed
        corr[rows, :] = jnp.sum(total, axis=-1, keepdims=True) / inv
        inverse[rows, :] = inv
    for group in range(4):
        put(group).wait()


def input_kernel(idx, slopes, w0, w1, w2, w3, extra, before, own_a, par_a, out_b, last_a, last_b):
    step = pl.program_id(0)
    for q, w in enumerate((w0, w1, w2, w3)):
        part = lax.dot_general(
            slopes[...], w[...], (((1,), (1,)), ((), ())), preferred_element_type=F32
        ).astype(BF)
        at = lax.rem(idx[4 * step + q], NZ)
        own_a[0, at, :EXTRA, :] = extra[0]
        own_a[0, at, EXTRA:, :] = part[:OUT_A]
        for out_a in (par_a.at[0], last_a):
            out_a[at, :EXTRA, :] = extra[1]
            out_a[at, EXTRA:, :] = part[TOK : TOK + OUT_A]
        for m in range(2):
            rows = part[m * TOK + OUT_A : (m + 1) * TOK]
            out_b[q, m] = rows
            if q == 0:
                last_b[m] = rows


def weight_kernel(idx, x0, x1, x2, x3, ready, *refs):
    got, out = refs[:-1], refs[-1]
    for q, x in enumerate((x0, x1, x2, x3)):
        part = lax.dot_general(
            x[...], ready[...], (((0,), (0,)), ((), ())), preferred_element_type=F32
        )
        out[q] = (part + got[0][q].astype(F32) if got else part).astype(BF)


MIB = 1024 * 1024


def _params():
    return pltpu.CompilerParams(dimension_semantics=("arbitrary",), vmem_limit_bytes=56 * MIB)


def _cost(flops, moved, exps=0):
    return pl.CostEstimate(flops=flops, bytes_accessed=moved, transcendentals=exps)


def _still(*shape):
    return pl.BlockSpec(shape, lambda *_: (0,) * len(shape))


def forward(idx, pieces, weights, grad):
    smem = pl.BlockSpec(memory_space=pltpu.SMEM)
    vmem = pl.BlockSpec(memory_space=pltpu.VMEM)
    hbm = pl.BlockSpec(memory_space=pltpu.HBM)
    return pl.pallas_call(
        forward_kernel,
        in_specs=[smem, *[hbm] * (PIECES + 1), vmem],
        out_specs=[pl.BlockSpec(memory_space=pl.ANY), *[vmem] * 4],
        scratch_shapes=[
            pltpu.VMEM((2 * TOK, UNITS), F32),
            pltpu.VMEM((2 * TOK, 128), F32),
            pltpu.VMEM((FEATS, UNITS), BF),
            pltpu.SemaphoreType.DMA((16,)),
            *[pltpu.VMEM(piece.shape, BF) for piece in pieces],
            pltpu.SemaphoreType.DMA((PIECES,)),
            pltpu.VMEM((2 * TOK, FEATS), BF),
            pltpu.SemaphoreType.DMA((4,)),
        ],
        out_shape=[
            jax.ShapeDtypeStruct((2 * TOK, FEATS), BF),
            jax.ShapeDtypeStruct((2 * TOK, UNITS), BF),
            jax.ShapeDtypeStruct((2 * TOK, UNITS), BF),
            jax.ShapeDtypeStruct((2 * TOK, 1), F32),
            jax.ShapeDtypeStruct((2 * TOK, 1), F32),
        ],
        compiler_params=pltpu.CompilerParams(vmem_limit_bytes=52 * MIB),
        cost_estimate=_cost(2 * 640 * FEATS * UNITS, 14 << 20, 640 * 512),
        name="forward_slopes",
    )(idx, *pieces, weights, grad)


def input_parts(idx, slopes, weights, extra, before):
    return pl.pallas_call(
        input_kernel,
        grid_spec=pltpu.PrefetchScalarGridSpec(
            num_scalar_prefetch=1,
            grid=(4,),
            in_specs=[
                _still(2 * TOK, UNITS),
                *[
                    pl.BlockSpec((BLK, UNITS), lambda k, i, q=q: (i[4 * k + q], 0))
                    for q in range(4)
                ],
                _still(2, EXTRA, BLK),
                pl.BlockSpec(memory_space=pl.ANY),
            ],
            out_specs=[
                pl.BlockSpec((1, NZ, EXTRA + OUT_A, BLK), lambda k, i: (i[16 + k // 2], 0, 0, 0)),
                pl.BlockSpec((1, NZ, EXTRA + OUT_A, BLK), lambda k, i: (k // 2, 0, 0, 0)),
                pl.BlockSpec((4, 2, TOK - OUT_A, BLK), lambda k, i: (k % 2, i[16 + k // 2], 0, 0)),
                _still(NZ, EXTRA + OUT_A, BLK),
                pl.BlockSpec((2, TOK - OUT_A, BLK), lambda k, i: (i[16 + k // 2], 0, 0)),
            ],
        ),
        out_shape=[
            *[jax.ShapeDtypeStruct((2, NZ, EXTRA + OUT_A, BLK), BF)] * 2,
            jax.ShapeDtypeStruct((NZ, 4, TOK - OUT_A, BLK), BF),
            jax.ShapeDtypeStruct((NZ, EXTRA + OUT_A, BLK), BF),
            jax.ShapeDtypeStruct((4, TOK - OUT_A, BLK), BF),
        ],
        compiler_params=_params(),
        cost_estimate=_cost(2 * 640 * FEATS * UNITS, 14 << 20),
        name="input_parts",
    )(idx, slopes, *[weights] * 4, extra, before)


def weight_parts(idx, scaled, ready, *got):
    blocks = pl.BlockSpec((4, BLK, UNITS), lambda s, i: (s, 0, 0))
    return pl.pallas_call(
        weight_kernel,
        grid_spec=pltpu.PrefetchScalarGridSpec(
            num_scalar_prefetch=1,
            grid=(2,),
            in_specs=[
                *[
                    pl.BlockSpec((2 * TOK, BLK), lambda s, i, q=q: (0, i[4 * s + q]))
                    for q in range(4)
                ],
                _still(2 * TOK, UNITS),
                *[blocks] * len(got),
            ],
            out_specs=blocks,
        ),
        out_shape=jax.ShapeDtypeStruct((8, BLK, UNITS), BF),
        compiler_params=_params(),
        cost_estimate=_cost(640 * FEATS * UNITS, 7 << 20),
        name="weight_parts",
    )(idx, *[scaled] * 4, ready, *got)


def gather_plane(shard, gain, pair):
    high = gain.astype(BF)
    low = (gain - high.astype(F32)).astype(BF)
    head = jnp.concatenate([high[None], low[None], jnp.zeros((EXTRA - 2, BLK), BF)], axis=0)
    part_a = jnp.concatenate([head, shard[:IN_A]], axis=0)
    part_b = shard[IN_A:]
    rows = {0: jnp.stack([part_b] + [move(part_b, flip=j) for j in (1, 2, 3)])}
    line = swap_z(jnp.broadcast_to(part_a, (NZ, *part_a.shape)))
    rows[1], rows[7] = move(rows[0], dz=-1, turn=True), move(rows[0], dz=1, turn=True)
    line = after(line, pair)
    twin, cross = move(line, flip=1), move(line, flip=3)
    rows[1], rows[7] = after((rows[1], rows[7]), line)
    for p in (2, 3):
        rows[p] = move(rows[p - 1], dz=-1, turn=True)
        rows[8 - p] = move(rows[(9 - p) % 8], dz=1, turn=True)
    rows[4] = move(rows[3], dz=-1, turn=True)
    upper, lower = move(twin[:, :CUT], flip=3), move(cross[:, CUT:], flip=1)
    return [line, twin, upper, lower, cross] + [rows[p] for p in range(NZ)]


def pick(first, second, d):
    return jnp.where(d == 0, first, second)


def mine(left, right, d):
    rest = FULL + 2 * HALF
    return jnp.concatenate(
        [
            pick(left[:, :FULL], left[:, rest:], d),
            pick(left[:, FULL : FULL + HALF], left[:, FULL + HALF : rest], d),
            pick(right[:, FULL : FULL + HALF], right[:, FULL + HALF : rest], d),
            pick(right[:, :FULL], right[:, rest:], d),
        ],
        axis=1,
    )


def tables():
    tensor, fsdp, d = (lax.axis_index(axis).astype(jnp.int32) for axis in AXES)
    y_hi, z = tensor // NZ, tensor % NZ
    x, c = fsdp // 2, fsdp % 2
    k = jnp.arange(16, dtype=jnp.int32)
    block = ((y_hi + k // 8) % 2) * NZ + (z + (1 - 2 * c) * (k % 8)) % NZ
    halves = jnp.stack([d ^ c, 1 - (d ^ c)])
    order = jnp.concatenate([jnp.where(d ^ c == 0, block, jnp.roll(block, NZ)), halves])

    def of_core(core):
        s = jnp.arange(8, dtype=jnp.int32)
        to = x + (1 - 2 * core) * (s // 2)
        g = ((to % NX) * 2 + core) * 2 + s % 2
        h, p = (g // NZ - y_hi) % 2, ((1 - 2 * c) * (g % NZ - z)) % NZ
        return h * NZ + p

    return block, order, of_core(1 - c), of_core(c), d


def body(inputs, norm_gain, gate_weight, up_weight, hidden_grad):
    block, order, other_core, this_core, d = tables()
    weights = lax.all_gather(mine(gate_weight, up_weight, d), "fsdp", axis=0, tiled=True)

    grad = hidden_grad[0]
    keep = mine(grad, grad, d)[:, : FULL + 128]
    give = mine(grad, grad, 1 - d)[:, : FULL + 128]
    received = move(give, flip=1)
    grads = jnp.concatenate([keep, received], axis=0)

    local_x = inputs[0]
    pieces = gather_plane(local_x, norm_gain, received)
    scaled, slopes, ready, corr, inverse = forward(block, pieces, weights, grads)

    rows = jnp.pad(corr.reshape(2, TOK) / FEATS, ((0, 0), (0, 512 - TOK))).reshape(2, 2, BLK)
    extra = jnp.pad(rows, ((0, 0), (0, EXTRA - 2), (0, 0))).astype(BF)
    own_a, par_a, part_b, last_a, last_b = input_parts(order, slopes, weights, extra, ready)
    ring_y = move(last_a, dy=1, turn=True)
    up = move(last_b, dz=1, turn=True)
    theirs = weight_parts(other_core, scaled, after(ready, part_b))

    ring_y, up = after((ring_y, up), theirs)
    got = move(after(theirs, ring_y, up), dc=1)
    ring_y = add(own_a[1], ring_y).astype(BF)
    up, down = add(part_b[3], up).astype(BF), part_b[5]
    ring_y, up, down = after((ring_y, up, down))
    ours = weight_parts(this_core, scaled, after(ready, ring_y, up), got)
    parts = [ours[2 * k : 2 * k + 2] for k in range(NX)]
    ring_y = move(ring_y, dy=1, turn=True)
    up, down = move(up, dz=1, turn=True), move(down, dz=-1, turn=True)

    ring_y, up, down = after((ring_y, up, down), ours)
    ring_y = add(par_a[0], ring_y).astype(BF)
    up, down = add(part_b[2], up).astype(BF), add(part_b[6], down).astype(BF)
    ring_y, up, down = after((ring_y, up, down))
    x_next = move(parts[1], dx=1, turn=True)
    ring_y = move(ring_y, dy=1, turn=True)
    up, down = move(up, dz=1, turn=True), move(down, dz=-1, turn=True)

    line = add(own_a[0], ring_y).astype(BF)
    up, down = add(part_b[1], up).astype(BF), add(part_b[7], down).astype(BF)
    line, up, down, far_x, last_x = after((line, up, down, parts[2], parts[3]), x_next)
    up, down = move(up, dz=1, turn=True), move(down, dz=-1, turn=True)
    line = swap_z(line)
    x_across, x_back = move(far_x, dx=2), move(last_x, dx=-1, turn=True)

    column = add(part_b[0], up, down)
    sent = column.astype(BF)
    sum_b = add(column[0], *[move(sent[j], flip=j) for j in (1, 2, 3)])
    sum_a = jnp.sum(line.astype(F32), axis=0)
    x_across, x_back = after((x_across, x_back), sum_b)
    rows = add(parts[0], x_next, x_across, x_back)
    rows_0, rows_1 = rows[0], rows[1]
    keep = pick(rows_0, rows_1, d).astype(BF)
    got = move(pick(rows_1, rows_0, d).astype(BF), flip=1)

    def whole(start, shared):
        left, right = pick(keep, got, d), pick(got, keep, d)
        return jnp.concatenate(
            [
                left[:, start : start + FULL],
                left[:, shared : shared + HALF],
                right[:, shared : shared + HALF],
                right[:, start : start + FULL],
            ],
            axis=1,
        )

    gate_grad = whole(0, FULL)
    up_grad = whole(FULL + 128, FULL + HALF)

    normed_grad = jnp.concatenate([sum_a[EXTRA:], sum_b], axis=0)
    correction = sum_a[:2].reshape(512)[:TOK][:, None]
    inv = inverse[:TOK]
    x = local_x.astype(F32)
    input_grad = inv * (normed_grad * norm_gain) - x * inv * inv * inv * correction
    gain_part = jnp.sum(normed_grad * x * inv, axis=0).reshape(2, 128)
    gain_part = gain_part + move(gain_part, dc=1)
    gain_part = (
        gain_part + move(gain_part, dx=1) + move(gain_part, dx=-1) + move(gain_part, dx=2)
    )
    gain_grad = (gain_part + move(gain_part, flip=1)).reshape(BLK)
    return input_grad.astype(BF)[None], gain_grad, gate_grad, up_grad


def solution(mesh):
    placed = (
        P(("fsdp", "dp"), None, "tensor"),
        P("tensor"),
        P("fsdp", "tensor"),
        P("fsdp", "tensor"),
        P(("fsdp", "dp"), None, "tensor"),
    )
    return jax.shard_map(
        body,
        mesh=mesh,
        in_specs=placed,
        out_specs=(
            P(("fsdp", "dp"), None, "tensor"),
            P("tensor"),
            P(("fsdp", "dp"), "tensor"),
            P(("fsdp", "dp"), "tensor"),
        ),
        check_vma=False,
    )
```

```python
import jax
import jax.numpy as jnp
from jax import lax
from jax.experimental import pallas as pl
from jax.experimental.pallas import tpu as pltpu
from jax.sharding import PartitionSpec as P

norm_epsilon = 1e-05
AXES = ("tensor", "fsdp", "dp")
NX, NY, NZ = 4, 4, 8
BF = jnp.bfloat16
F32 = jnp.float32
TOK = 320
BLK = 256
FEATS = 4096
UNITS = 896
EXTRA = 16
IN_A = 160
OUT_A = 128
CUT = 96
FULL = 384
HALF = 64


def _index(x, c, y, z):
    return (((y % NY) // 2) * NZ + z % NZ) * 16 + ((x % NX) * 2 + c % 2) * 2 + y % 2


def _pairs(dx=0, dc=0, dy=0, dz=0, flip=0, turn=False):
    pairs = []
    for x in range(NX):
        for c in range(2):
            way = -1 if turn and c else 1
            for y in range(NY):
                for z in range(NZ):
                    to = (y ^ flip) + way * dy
                    there = _index(x + way * dx, c + dc, to, z + way * dz)
                    pairs.append((_index(x, c, y, z), there))
    return pairs


def move(value, **step):
    return lax.ppermute(value, AXES, _pairs(**step))


def swap_z(blocks):
    lines = [[half * NZ + z for z in range(NZ)] for half in range(2)]
    return lax.all_to_all(
        blocks, "tensor", split_axis=0, concat_axis=0, tiled=True, axis_index_groups=lines
    )


def after(value, *others):
    return lax.optimization_barrier((value, *others))[0]


def add(*terms):
    total = terms[0].astype(F32)
    for term in terms[1:]:
        total = total + term.astype(F32)
    return total


PIECES = 13
CHUNK = 64


def forward_kernel(idx, *refs):
    w, grad, scaled_out, slopes, ready, corr, inverse = refs[PIECES : PIECES + 7]
    acc, square, held, sems, *here = refs[PIECES + 7 : 2 * PIECES + 11]
    piece_sems, scaled, out_sems = refs[2 * PIECES + 11 :]
    line, twin, upper, lower, cross = here[:5]
    pieces_a = ([line], [twin], [upper, lower], [cross])
    pieces_b = here[5:]

    def fetch(k):
        there = pl.ds(pl.multiple_of(idx[k] * BLK, BLK), BLK)
        return pltpu.make_async_copy(w.at[there], held.at[pl.ds(k * BLK, BLK)], sems.at[k])

    def bring(i):
        return pltpu.make_async_copy(refs[i], here[i], piece_sems.at[i])

    def put(group):
        lanes = pl.ds(4 * group * BLK, 4 * BLK)
        return pltpu.make_async_copy(scaled.at[:, lanes], scaled_out.at[:, lanes], out_sems.at[group])

    needed = ((0, 1, 5, 6, 7, 8), (9, 10, 11, 12), (2, 3, 4), ())
    for group in range(4):
        for i in needed[group]:
            bring(i).start()
        for k in range(4 * group, 4 * group + 4):
            fetch(k).start()
    square[...] = jnp.zeros_like(square)
    for group in range(4):
        h, quad = group // 2, group % 2
        for i in needed[group]:
            bring(i).wait()
        for m in range(2):
            j = 2 * h + m
            sums_a, sums_b = [], []
            for q in range(4):
                p = 4 * quad + q
                lanes = pl.ds((4 * group + q) * BLK, BLK)
                at = lax.rem(idx[8 * h + p], NZ)
                head = pieces_a[j][0][at, 0:EXTRA, :].astype(F32)
                gain = head[0:1] + head[1:2]
                row, skip = m * TOK, EXTRA
                for piece in pieces_a[j]:
                    x = piece[at, skip:, :].astype(F32)
                    scaled[pl.ds(row, x.shape[0]), lanes] = (x * gain).astype(BF)
                    sq = x * x
                    sums_a.append((row, sq[:, :128] + sq[:, 128:]))
                    row, skip = row + x.shape[0], 0
                x = pieces_b[p][j].astype(F32)
                scaled[pl.ds(m * TOK + IN_A, TOK - IN_A), lanes] = (x * gain).astype(BF)
                sq = x * x
                sums_b.append(sq[:, :128] + sq[:, 128:])
            for row in sorted({row for row, _ in sums_a}):
                terms = [sq for at, sq in sums_a if at == row]
                square[pl.ds(row, terms[0].shape[0]), :] += sum(terms[1:], terms[0])
            square[pl.ds(m * TOK + IN_A, TOK - IN_A), :] += sum(sums_b[1:], sums_b[0])
        for q in range(4):
            fetch(4 * group + q).wait()
        put(group).start()
        lanes = pl.ds(4 * group * BLK, 4 * BLK)
        product = jnp.dot(scaled[:, lanes], held[lanes, :], preferred_element_type=F32)
        acc[...] = product if group == 0 else acc[...] + product

    first = lax.broadcasted_iota(jnp.int32, (CHUNK, 128), 1) < HALF

    def slope_pair(gate, up, upstream):
        s = 1.0 / (1.0 + jnp.exp(-gate))
        return upstream * up * s * (1.0 + gate * (1.0 - s)), upstream * gate * s

    for chunk in range(2 * TOK // CHUNK):
        rows = pl.ds(chunk * CHUNK, CHUNK)
        mean = jnp.sum(square[rows, :], axis=-1, keepdims=True) / FEATS
        inv = lax.rsqrt(mean + norm_epsilon)
        total = jnp.zeros((CHUNK, 128), F32)
        for tile in range(FULL // 128):
            here, there = pl.ds(tile * 128, 128), pl.ds(FULL + 128 + tile * 128, 128)
            gate, up = acc[rows, here] * inv, acc[rows, there] * inv
            down, lift = slope_pair(gate, up, grad[rows, here].astype(F32))
            slopes[rows, here] = down.astype(BF)
            slopes[rows, there] = lift.astype(BF)
            ready[rows, here] = (down * inv).astype(BF)
            ready[rows, there] = (lift * inv).astype(BF)
            total += down * gate + lift * up
        here = pl.ds(FULL, 128)
        mixed = acc[rows, here] * inv
        turned = pltpu.roll(mixed, HALF, 1)
        gate, up = jnp.where(first, mixed, turned), jnp.where(first, turned, mixed)
        down, lift = slope_pair(gate, up, grad[rows, here].astype(F32))
        both = jnp.where(first, down, lift)
        slopes[rows, here] = both.astype(BF)
        ready[rows, here] = (both * inv).astype(BF)
        total += both * mixed
        corr[rows, :] = jnp.sum(total, axis=-1, keepdims=True) / inv
        inverse[rows, :] = inv
    for group in range(4):
        put(group).wait()


def input_kernel(idx, slopes, w0, w1, w2, w3, extra, before, own_a, par_a, out_b, last_a, last_b):
    step = pl.program_id(0)
    for q, w in enumerate((w0, w1, w2, w3)):
        part = lax.dot_general(
            slopes[...], w[...], (((1,), (1,)), ((), ())), preferred_element_type=F32
        ).astype(BF)
        at = lax.rem(idx[4 * step + q], NZ)
        own_a[0, at, :EXTRA, :] = extra[0]
        own_a[0, at, EXTRA:, :] = part[:OUT_A]
        for out_a in (par_a.at[0], last_a):
            out_a[at, :EXTRA, :] = extra[1]
            out_a[at, EXTRA:, :] = part[TOK : TOK + OUT_A]
        for m in range(2):
            rows = part[m * TOK + OUT_A : (m + 1) * TOK]
            out_b[q, m] = rows
            if q == 0:
                last_b[m] = rows


def weight_kernel(idx, x0, x1, x2, x3, ready, *refs):
    got, out = refs[:-1], refs[-1]
    for q, x in enumerate((x0, x1, x2, x3)):
        part = lax.dot_general(
            x[...], ready[...], (((0,), (0,)), ((), ())), preferred_element_type=F32
        )
        out[q] = (part + got[0][q].astype(F32) if got else part).astype(BF)


MIB = 1024 * 1024


def _params(grant=56):
    return pltpu.CompilerParams(
        dimension_semantics=("arbitrary",), vmem_limit_bytes=grant * MIB
    )


def _cost(flops, moved, exps=0):
    return pl.CostEstimate(flops=flops, bytes_accessed=moved, transcendentals=exps)


def _still(*shape):
    return pl.BlockSpec(shape, lambda *_: (0,) * len(shape))


def forward(idx, pieces, weights, grad):
    smem = pl.BlockSpec(memory_space=pltpu.SMEM)
    vmem = pl.BlockSpec(memory_space=pltpu.VMEM)
    hbm = pl.BlockSpec(memory_space=pltpu.HBM)
    return pl.pallas_call(
        forward_kernel,
        in_specs=[smem, *[hbm] * (PIECES + 1), vmem],
        out_specs=[pl.BlockSpec(memory_space=pl.ANY), *[vmem] * 4],
        scratch_shapes=[
            pltpu.VMEM((2 * TOK, UNITS), F32),
            pltpu.VMEM((2 * TOK, 128), F32),
            pltpu.VMEM((FEATS, UNITS), BF),
            pltpu.SemaphoreType.DMA((16,)),
            *[pltpu.VMEM(piece.shape, BF) for piece in pieces],
            pltpu.SemaphoreType.DMA((PIECES,)),
            pltpu.VMEM((2 * TOK, FEATS), BF),
            pltpu.SemaphoreType.DMA((4,)),
        ],
        out_shape=[
            jax.ShapeDtypeStruct((2 * TOK, FEATS), BF),
            jax.ShapeDtypeStruct((2 * TOK, UNITS), BF),
            jax.ShapeDtypeStruct((2 * TOK, UNITS), BF),
            jax.ShapeDtypeStruct((2 * TOK, 1), F32),
            jax.ShapeDtypeStruct((2 * TOK, 1), F32),
        ],
        compiler_params=pltpu.CompilerParams(vmem_limit_bytes=52 * MIB),
        cost_estimate=_cost(2 * 640 * FEATS * UNITS, 14 << 20, 640 * 512),
        name="forward_slopes",
    )(idx, *pieces, weights, grad)


def input_parts(idx, slopes, weights, extra, before):
    return pl.pallas_call(
        input_kernel,
        grid_spec=pltpu.PrefetchScalarGridSpec(
            num_scalar_prefetch=1,
            grid=(4,),
            in_specs=[
                _still(2 * TOK, UNITS),
                *[
                    pl.BlockSpec((BLK, UNITS), lambda k, i, q=q: (i[4 * k + q], 0))
                    for q in range(4)
                ],
                _still(2, EXTRA, BLK),
                pl.BlockSpec(memory_space=pl.ANY),
            ],
            out_specs=[
                pl.BlockSpec((1, NZ, EXTRA + OUT_A, BLK), lambda k, i: (i[16 + k // 2], 0, 0, 0)),
                pl.BlockSpec((1, NZ, EXTRA + OUT_A, BLK), lambda k, i: (k // 2, 0, 0, 0)),
                pl.BlockSpec((4, 2, TOK - OUT_A, BLK), lambda k, i: (k % 2, i[16 + k // 2], 0, 0)),
                _still(NZ, EXTRA + OUT_A, BLK),
                pl.BlockSpec((2, TOK - OUT_A, BLK), lambda k, i: (i[16 + k // 2], 0, 0)),
            ],
        ),
        out_shape=[
            *[jax.ShapeDtypeStruct((2, NZ, EXTRA + OUT_A, BLK), BF)] * 2,
            jax.ShapeDtypeStruct((NZ, 4, TOK - OUT_A, BLK), BF),
            jax.ShapeDtypeStruct((NZ, EXTRA + OUT_A, BLK), BF),
            jax.ShapeDtypeStruct((4, TOK - OUT_A, BLK), BF),
        ],
        compiler_params=_params(),
        cost_estimate=_cost(2 * 640 * FEATS * UNITS, 14 << 20),
        name="input_parts",
    )(idx, slopes, *[weights] * 4, extra, before)


def weight_parts(idx, scaled, ready, *got):
    blocks = pl.BlockSpec((4, BLK, UNITS), lambda s, i: (s, 0, 0))
    return pl.pallas_call(
        weight_kernel,
        grid_spec=pltpu.PrefetchScalarGridSpec(
            num_scalar_prefetch=1,
            grid=(2,),
            in_specs=[
                *[
                    pl.BlockSpec((2 * TOK, BLK), lambda s, i, q=q: (0, i[4 * s + q]))
                    for q in range(4)
                ],
                _still(2 * TOK, UNITS),
                *[blocks] * len(got),
            ],
            out_specs=blocks,
        ),
        out_shape=jax.ShapeDtypeStruct((8, BLK, UNITS), BF),
        compiler_params=_params(40 if got else 56),
        cost_estimate=_cost(640 * FEATS * UNITS, 7 << 20),
        name="weight_parts",
    )(idx, *[scaled] * 4, ready, *got)


def gather_plane(shard, gain, pair):
    high = gain.astype(BF)
    low = (gain - high.astype(F32)).astype(BF)
    head = jnp.concatenate([high[None], low[None], jnp.zeros((EXTRA - 2, BLK), BF)], axis=0)
    part_a = jnp.concatenate([head, shard[:IN_A]], axis=0)
    part_b = shard[IN_A:]
    rows = {0: jnp.stack([part_b] + [move(part_b, flip=j) for j in (1, 2, 3)])}
    line = swap_z(jnp.broadcast_to(part_a, (NZ, *part_a.shape)))
    rows[1], rows[7] = move(rows[0], dz=-1, turn=True), move(rows[0], dz=1, turn=True)
    line = after(line, pair)
    twin, cross = move(line, flip=1), move(line, flip=3)
    rows[1], rows[7] = after((rows[1], rows[7]), line)
    for p in (2, 3):
        rows[p] = move(rows[p - 1], dz=-1, turn=True)
        rows[8 - p] = move(rows[(9 - p) % 8], dz=1, turn=True)
    rows[4] = move(rows[3], dz=-1, turn=True)
    upper, lower = move(twin[:, :CUT], flip=3), move(cross[:, CUT:], flip=1)
    return [line, twin, upper, lower, cross] + [rows[p] for p in range(NZ)]


def pick(first, second, d):
    return jnp.where(d == 0, first, second)


def mine(left, right, d):
    rest = FULL + 2 * HALF
    return jnp.concatenate(
        [
            pick(left[:, :FULL], left[:, rest:], d),
            pick(left[:, FULL : FULL + HALF], left[:, FULL + HALF : rest], d),
            pick(right[:, FULL : FULL + HALF], right[:, FULL + HALF : rest], d),
            pick(right[:, :FULL], right[:, rest:], d),
        ],
        axis=1,
    )


def tables():
    tensor, fsdp, d = (lax.axis_index(axis).astype(jnp.int32) for axis in AXES)
    y_hi, z = tensor // NZ, tensor % NZ
    x, c = fsdp // 2, fsdp % 2
    k = jnp.arange(16, dtype=jnp.int32)
    block = ((y_hi + k // 8) % 2) * NZ + (z + (1 - 2 * c) * (k % 8)) % NZ
    halves = jnp.stack([d ^ c, 1 - (d ^ c)])
    order = jnp.concatenate([jnp.where(d ^ c == 0, block, jnp.roll(block, NZ)), halves])

    def of_core(core):
        s = jnp.arange(8, dtype=jnp.int32)
        to = x + (1 - 2 * core) * (s // 2)
        g = ((to % NX) * 2 + core) * 2 + s % 2
        h, p = (g // NZ - y_hi) % 2, ((1 - 2 * c) * (g % NZ - z)) % NZ
        return h * NZ + p

    return block, order, of_core(1 - c), of_core(c), d


def body(inputs, norm_gain, gate_weight, up_weight, hidden_grad):
    block, order, other_core, this_core, d = tables()
    weights = lax.all_gather(mine(gate_weight, up_weight, d), "fsdp", axis=0, tiled=True)

    grad = hidden_grad[0]
    keep = mine(grad, grad, d)[:, : FULL + 128]
    give = mine(grad, grad, 1 - d)[:, : FULL + 128]
    received = move(give, flip=1)
    grads = jnp.concatenate([keep, received], axis=0)

    local_x = inputs[0]
    pieces = gather_plane(local_x, norm_gain, received)
    scaled, slopes, ready, corr, inverse = forward(block, pieces, weights, grads)

    rows = jnp.pad(corr.reshape(2, TOK) / FEATS, ((0, 0), (0, 512 - TOK))).reshape(2, 2, BLK)
    extra = jnp.pad(rows, ((0, 0), (0, EXTRA - 2), (0, 0))).astype(BF)
    own_a, par_a, part_b, last_a, last_b = input_parts(order, slopes, weights, extra, ready)
    ring_y = move(last_a, dy=1, turn=True)
    up = move(last_b, dz=1, turn=True)
    theirs = weight_parts(other_core, scaled, after(ready, part_b))

    ring_y, up = after((ring_y, up), theirs)
    got = move(after(theirs, ring_y, up), dc=1)
    ring_y = add(own_a[1], ring_y).astype(BF)
    up, down = add(part_b[3], up).astype(BF), part_b[5]
    ring_y, up, down = after((ring_y, up, down))
    ours = weight_parts(this_core, scaled, after(ready, ring_y, up), got)
    parts = [ours[2 * k : 2 * k + 2] for k in range(NX)]
    ring_y = move(ring_y, dy=1, turn=True)
    up, down = move(up, dz=1, turn=True), move(down, dz=-1, turn=True)

    ring_y, up, down = after((ring_y, up, down), ours)
    ring_y = add(par_a[0], ring_y).astype(BF)
    up, down = add(part_b[2], up).astype(BF), add(part_b[6], down).astype(BF)
    ring_y, up, down = after((ring_y, up, down))
    x_next = move(parts[1], dx=1, turn=True)
    ring_y = move(ring_y, dy=1, turn=True)
    up, down = move(up, dz=1, turn=True), move(down, dz=-1, turn=True)

    line = add(own_a[0], ring_y).astype(BF)
    up, down = add(part_b[1], up).astype(BF), add(part_b[7], down).astype(BF)
    line, up, down, far_x, last_x = after((line, up, down, parts[2], parts[3]), x_next)
    up, down = move(up, dz=1, turn=True), move(down, dz=-1, turn=True)
    line = swap_z(line)
    x_across, x_back = move(far_x, dx=2), move(last_x, dx=-1, turn=True)

    column = add(part_b[0], up, down)
    sent = column.astype(BF)
    sum_b = add(column[0], *[move(sent[j], flip=j) for j in (1, 2, 3)])
    sum_a = jnp.sum(line.astype(F32), axis=0)
    x_across, x_back = after((x_across, x_back), sum_b)
    rows = add(parts[0], x_next, x_across, x_back)
    rows_0, rows_1 = rows[0], rows[1]
    keep = pick(rows_0, rows_1, d).astype(BF)
    got = move(pick(rows_1, rows_0, d).astype(BF), flip=1)

    def whole(start, shared):
        left, right = pick(keep, got, d), pick(got, keep, d)
        return jnp.concatenate(
            [
                left[:, start : start + FULL],
                left[:, shared : shared + HALF],
                right[:, shared : shared + HALF],
                right[:, start : start + FULL],
            ],
            axis=1,
        )

    gate_grad = whole(0, FULL)
    up_grad = whole(FULL + 128, FULL + HALF)

    normed_grad = jnp.concatenate([sum_a[EXTRA:], sum_b], axis=0)
    correction = sum_a[:2].reshape(512)[:TOK][:, None]
    inv = inverse[:TOK]
    x = local_x.astype(F32)
    input_grad = inv * (normed_grad * norm_gain) - x * inv * inv * inv * correction
    gain_part = jnp.sum(normed_grad * x * inv, axis=0).reshape(2, 128)
    gain_part = gain_part + move(gain_part, dc=1)
    gain_part = (
        gain_part + move(gain_part, dx=1) + move(gain_part, dx=-1) + move(gain_part, dx=2)
    )
    gain_grad = (gain_part + move(gain_part, flip=1)).reshape(BLK)
    return input_grad.astype(BF)[None], gain_grad, gate_grad, up_grad


def solution(mesh):
    placed = (
        P(("fsdp", "dp"), None, "tensor"),
        P("tensor"),
        P("fsdp", "tensor"),
        P("fsdp", "tensor"),
        P(("fsdp", "dp"), None, "tensor"),
    )
    return jax.shard_map(
        body,
        mesh=mesh,
        in_specs=placed,
        out_specs=(
            P(("fsdp", "dp"), None, "tensor"),
            P("tensor"),
            P(("fsdp", "dp"), "tensor"),
            P(("fsdp", "dp"), "tensor"),
        ),
        check_vma=False,
    )
```

```python
import jax
import jax.numpy as jnp
from jax import lax
from jax.experimental import pallas as pl
from jax.experimental.pallas import tpu as pltpu
from jax.sharding import PartitionSpec as P

norm_epsilon = 1e-05
AXES = ("tensor", "fsdp", "dp")
NX, NY, NZ = 4, 4, 8
BF = jnp.bfloat16
F32 = jnp.float32
TOK = 320
BLK = 256
FEATS = 4096
UNITS = 896
EXTRA = 16
IN_A = 160
OUT_A = 128
CUT = 96
FULL = 384
HALF = 64


def _index(x, c, y, z):
    return (((y % NY) // 2) * NZ + z % NZ) * 16 + ((x % NX) * 2 + c % 2) * 2 + y % 2


def _pairs(dx=0, dc=0, dy=0, dz=0, flip=0, turn=False):
    pairs = []
    for x in range(NX):
        for c in range(2):
            way = -1 if turn and c else 1
            for y in range(NY):
                for z in range(NZ):
                    to = (y ^ flip) + way * dy
                    there = _index(x + way * dx, c + dc, to, z + way * dz)
                    pairs.append((_index(x, c, y, z), there))
    return pairs


def move(value, **step):
    return lax.ppermute(value, AXES, _pairs(**step))


def swap_z(blocks):
    lines = [[half * NZ + z for z in range(NZ)] for half in range(2)]
    return lax.all_to_all(
        blocks, "tensor", split_axis=0, concat_axis=0, tiled=True, axis_index_groups=lines
    )


def after(value, *others):
    return lax.optimization_barrier((value, *others))[0]


def add(*terms):
    total = terms[0].astype(F32)
    for term in terms[1:]:
        total = total + term.astype(F32)
    return total


PIECES = 13
CHUNK = 64


def forward_kernel(idx, *refs):
    w, grad, scaled_out, slopes, ready, corr, inverse = refs[PIECES : PIECES + 7]
    acc, square, held, sems, *here = refs[PIECES + 7 : 2 * PIECES + 11]
    piece_sems, scaled, out_sems = refs[2 * PIECES + 11 :]
    line, twin, upper, lower, cross = here[:5]
    pieces_a = ([line], [twin], [upper, lower], [cross])
    pieces_b = here[5:]

    def fetch(k):
        there = pl.ds(pl.multiple_of(idx[k] * BLK, BLK), BLK)
        return pltpu.make_async_copy(w.at[there], held.at[pl.ds(k * BLK, BLK)], sems.at[k])

    def bring(i):
        return pltpu.make_async_copy(refs[i], here[i], piece_sems.at[i])

    def put(group):
        lanes = pl.ds(4 * group * BLK, 4 * BLK)
        return pltpu.make_async_copy(scaled.at[:, lanes], scaled_out.at[:, lanes], out_sems.at[group])

    needed = ((0, 1, 5, 6, 7, 8), (9, 10, 11, 12), (2, 3, 4), ())
    for group in range(4):
        for i in needed[group]:
            bring(i).start()
        for k in range(4 * group, 4 * group + 4):
            fetch(k).start()
    square[...] = jnp.zeros_like(square)
    for group in range(4):
        h, quad = group // 2, group % 2
        for i in needed[group]:
            bring(i).wait()
        for m in range(2):
            j = 2 * h + m
            sums_a, sums_b = [], []
            for q in range(4):
                p = 4 * quad + q
                lanes = pl.ds((4 * group + q) * BLK, BLK)
                at = lax.rem(idx[8 * h + p], NZ)
                head = pieces_a[j][0][at, 0:EXTRA, :].astype(F32)
                gain = head[0:1] + head[1:2]
                row, skip = m * TOK, EXTRA
                for piece in pieces_a[j]:
                    x = piece[at, skip:, :].astype(F32)
                    scaled[pl.ds(row, x.shape[0]), lanes] = (x * gain).astype(BF)
                    sq = x * x
                    sums_a.append((row, sq[:, :128] + sq[:, 128:]))
                    row, skip = row + x.shape[0], 0
                x = pieces_b[p][j].astype(F32)
                scaled[pl.ds(m * TOK + IN_A, TOK - IN_A), lanes] = (x * gain).astype(BF)
                sq = x * x
                sums_b.append(sq[:, :128] + sq[:, 128:])
            for row in sorted({row for row, _ in sums_a}):
                terms = [sq for at, sq in sums_a if at == row]
                square[pl.ds(row, terms[0].shape[0]), :] += sum(terms[1:], terms[0])
            square[pl.ds(m * TOK + IN_A, TOK - IN_A), :] += sum(sums_b[1:], sums_b[0])
        for q in range(4):
            fetch(4 * group + q).wait()
        put(group).start()
        lanes = pl.ds(4 * group * BLK, 4 * BLK)
        product = jnp.dot(scaled[:, lanes], held[lanes, :], preferred_element_type=F32)
        acc[...] = product if group == 0 else acc[...] + product

    first = lax.broadcasted_iota(jnp.int32, (CHUNK, 128), 1) < HALF

    def slope_pair(gate, up, upstream):
        s = 1.0 / (1.0 + jnp.exp(-gate))
        return upstream * up * s * (1.0 + gate * (1.0 - s)), upstream * gate * s

    for chunk in range(2 * TOK // CHUNK):
        rows = pl.ds(chunk * CHUNK, CHUNK)
        mean = jnp.sum(square[rows, :], axis=-1, keepdims=True) / FEATS
        inv = lax.rsqrt(mean + norm_epsilon)
        total = jnp.zeros((CHUNK, 128), F32)
        for tile in range(FULL // 128):
            here, there = pl.ds(tile * 128, 128), pl.ds(FULL + 128 + tile * 128, 128)
            gate, up = acc[rows, here] * inv, acc[rows, there] * inv
            down, lift = slope_pair(gate, up, grad[rows, here].astype(F32))
            slopes[rows, here] = down.astype(BF)
            slopes[rows, there] = lift.astype(BF)
            ready[rows, here] = (down * inv).astype(BF)
            ready[rows, there] = (lift * inv).astype(BF)
            total += down * gate + lift * up
        here = pl.ds(FULL, 128)
        mixed = acc[rows, here] * inv
        turned = pltpu.roll(mixed, HALF, 1)
        gate, up = jnp.where(first, mixed, turned), jnp.where(first, turned, mixed)
        down, lift = slope_pair(gate, up, grad[rows, here].astype(F32))
        both = jnp.where(first, down, lift)
        slopes[rows, here] = both.astype(BF)
        ready[rows, here] = (both * inv).astype(BF)
        total += both * mixed
        corr[rows, :] = jnp.sum(total, axis=-1, keepdims=True) / inv
        inverse[rows, :] = inv
    for group in range(4):
        put(group).wait()


def input_kernel(idx, slopes, w0, w1, w2, w3, extra, before, own_a, par_a, out_b, last_a, last_b):
    step = pl.program_id(0)
    for q, w in enumerate((w0, w1, w2, w3)):
        part = lax.dot_general(
            slopes[...], w[...], (((1,), (1,)), ((), ())), preferred_element_type=F32
        ).astype(BF)
        at = lax.rem(idx[4 * step + q], NZ)
        own_a[0, at, :EXTRA, :] = extra[0]
        own_a[0, at, EXTRA:, :] = part[:OUT_A]
        for out_a in (par_a.at[0], last_a):
            out_a[at, :EXTRA, :] = extra[1]
            out_a[at, EXTRA:, :] = part[TOK : TOK + OUT_A]
        for m in range(2):
            rows = part[m * TOK + OUT_A : (m + 1) * TOK]
            out_b[q, m] = rows
            if q == 0:
                last_b[m] = rows


def weight_kernel(idx, x0, x1, x2, x3, ready, *refs):
    got, out = refs[:-1], refs[-1]
    for q, x in enumerate((x0, x1, x2, x3)):
        part = lax.dot_general(
            x[...], ready[...], (((0,), (0,)), ((), ())), preferred_element_type=F32
        )
        out[q] = (part + got[0][q].astype(F32) if got else part).astype(BF)


MIB = 1024 * 1024


def _params(grant=56):
    return pltpu.CompilerParams(
        dimension_semantics=("arbitrary",), vmem_limit_bytes=grant * MIB
    )


def _cost(flops, moved, exps=0):
    return pl.CostEstimate(flops=flops, bytes_accessed=moved, transcendentals=exps)


def _still(*shape):
    return pl.BlockSpec(shape, lambda *_: (0,) * len(shape))


def forward(idx, pieces, weights, grad):
    smem = pl.BlockSpec(memory_space=pltpu.SMEM)
    vmem = pl.BlockSpec(memory_space=pltpu.VMEM)
    hbm = pl.BlockSpec(memory_space=pltpu.HBM)
    return pl.pallas_call(
        forward_kernel,
        in_specs=[smem, *[hbm] * (PIECES + 1), vmem],
        out_specs=[pl.BlockSpec(memory_space=pl.ANY), *[vmem] * 4],
        scratch_shapes=[
            pltpu.VMEM((2 * TOK, UNITS), F32),
            pltpu.VMEM((2 * TOK, 128), F32),
            pltpu.VMEM((FEATS, UNITS), BF),
            pltpu.SemaphoreType.DMA((16,)),
            *[pltpu.VMEM(piece.shape, BF) for piece in pieces],
            pltpu.SemaphoreType.DMA((PIECES,)),
            pltpu.VMEM((2 * TOK, FEATS), BF),
            pltpu.SemaphoreType.DMA((4,)),
        ],
        out_shape=[
            jax.ShapeDtypeStruct((2 * TOK, FEATS), BF),
            jax.ShapeDtypeStruct((2 * TOK, UNITS), BF),
            jax.ShapeDtypeStruct((2 * TOK, UNITS), BF),
            jax.ShapeDtypeStruct((2 * TOK, 1), F32),
            jax.ShapeDtypeStruct((2 * TOK, 1), F32),
        ],
        compiler_params=pltpu.CompilerParams(vmem_limit_bytes=52 * MIB),
        cost_estimate=_cost(2 * 640 * FEATS * UNITS, 14 << 20, 640 * 512),
        name="forward_slopes",
    )(idx, *pieces, weights, grad)


def input_parts(idx, slopes, weights, extra, before):
    return pl.pallas_call(
        input_kernel,
        grid_spec=pltpu.PrefetchScalarGridSpec(
            num_scalar_prefetch=1,
            grid=(4,),
            in_specs=[
                _still(2 * TOK, UNITS),
                *[
                    pl.BlockSpec((BLK, UNITS), lambda k, i, q=q: (i[4 * k + q], 0))
                    for q in range(4)
                ],
                _still(2, EXTRA, BLK),
                pl.BlockSpec(memory_space=pl.ANY),
            ],
            out_specs=[
                pl.BlockSpec((1, NZ, EXTRA + OUT_A, BLK), lambda k, i: (i[16 + k // 2], 0, 0, 0)),
                pl.BlockSpec((1, NZ, EXTRA + OUT_A, BLK), lambda k, i: (k // 2, 0, 0, 0)),
                pl.BlockSpec((4, 2, TOK - OUT_A, BLK), lambda k, i: (k % 2, i[16 + k // 2], 0, 0)),
                _still(NZ, EXTRA + OUT_A, BLK),
                pl.BlockSpec((2, TOK - OUT_A, BLK), lambda k, i: (i[16 + k // 2], 0, 0)),
            ],
        ),
        out_shape=[
            *[jax.ShapeDtypeStruct((2, NZ, EXTRA + OUT_A, BLK), BF)] * 2,
            jax.ShapeDtypeStruct((NZ, 4, TOK - OUT_A, BLK), BF),
            jax.ShapeDtypeStruct((NZ, EXTRA + OUT_A, BLK), BF),
            jax.ShapeDtypeStruct((4, TOK - OUT_A, BLK), BF),
        ],
        compiler_params=_params(),
        cost_estimate=_cost(2 * 640 * FEATS * UNITS, 14 << 20),
        name="input_parts",
    )(idx, slopes, *[weights] * 4, extra, before)


def weight_parts(idx, scaled, ready, *got):
    blocks = pl.BlockSpec((4, BLK, UNITS), lambda s, i: (s, 0, 0))
    return pl.pallas_call(
        weight_kernel,
        grid_spec=pltpu.PrefetchScalarGridSpec(
            num_scalar_prefetch=1,
            grid=(2,),
            in_specs=[
                *[
                    pl.BlockSpec((2 * TOK, BLK), lambda s, i, q=q: (0, i[4 * s + q]))
                    for q in range(4)
                ],
                _still(2 * TOK, UNITS),
                *[blocks] * len(got),
            ],
            out_specs=blocks,
        ),
        out_shape=jax.ShapeDtypeStruct((8, BLK, UNITS), BF),
        compiler_params=_params(40 if got else 56),
        cost_estimate=_cost(640 * FEATS * UNITS, 7 << 20),
        name="weight_parts",
    )(idx, *[scaled] * 4, ready, *got)


def gather_plane(shard, gain, pair):
    high = gain.astype(BF)
    low = (gain - high.astype(F32)).astype(BF)
    head = jnp.concatenate([high[None], low[None], jnp.zeros((EXTRA - 2, BLK), BF)], axis=0)
    part_a = jnp.concatenate([head, shard[:IN_A]], axis=0)
    part_b = shard[IN_A:]
    rows = {0: jnp.stack([part_b] + [move(part_b, flip=j) for j in (1, 2, 3)])}
    line = swap_z(jnp.broadcast_to(part_a, (NZ, *part_a.shape)))
    rows[1], rows[7] = move(rows[0], dz=-1, turn=True), move(rows[0], dz=1, turn=True)
    line = after(line, pair)
    twin, cross = move(line, flip=1), move(line, flip=3)
    rows[1], rows[7] = after((rows[1], rows[7]), line)
    for p in (2, 3):
        rows[p] = move(rows[p - 1], dz=-1, turn=True)
        rows[8 - p] = move(rows[(9 - p) % 8], dz=1, turn=True)
    upper, rest = move(twin[:, :CUT], flip=3), cross[:, CUT:]
    last, rest = after((rows[3], rest))
    rows[4], lower = move(last, dz=-1, turn=True), move(rest, flip=1)
    return [line, twin, upper, lower, cross] + [rows[p] for p in range(NZ)]


def pick(first, second, d):
    return jnp.where(d == 0, first, second)


def mine(left, right, d):
    rest = FULL + 2 * HALF
    return jnp.concatenate(
        [
            pick(left[:, :FULL], left[:, rest:], d),
            pick(left[:, FULL : FULL + HALF], left[:, FULL + HALF : rest], d),
            pick(right[:, FULL : FULL + HALF], right[:, FULL + HALF : rest], d),
            pick(right[:, :FULL], right[:, rest:], d),
        ],
        axis=1,
    )


def tables():
    tensor, fsdp, d = (lax.axis_index(axis).astype(jnp.int32) for axis in AXES)
    y_hi, z = tensor // NZ, tensor % NZ
    x, c = fsdp // 2, fsdp % 2
    k = jnp.arange(16, dtype=jnp.int32)
    block = ((y_hi + k // 8) % 2) * NZ + (z + (1 - 2 * c) * (k % 8)) % NZ
    halves = jnp.stack([d ^ c, 1 - (d ^ c)])
    order = jnp.concatenate([jnp.where(d ^ c == 0, block, jnp.roll(block, NZ)), halves])

    def of_core(core):
        s = jnp.arange(8, dtype=jnp.int32)
        to = x + (1 - 2 * core) * (s // 2)
        g = ((to % NX) * 2 + core) * 2 + s % 2
        h, p = (g // NZ - y_hi) % 2, ((1 - 2 * c) * (g % NZ - z)) % NZ
        return h * NZ + p

    return block, order, of_core(1 - c), of_core(c), d


def body(inputs, norm_gain, gate_weight, up_weight, hidden_grad):
    block, order, other_core, this_core, d = tables()
    weights = lax.all_gather(mine(gate_weight, up_weight, d), "fsdp", axis=0, tiled=True)

    grad = hidden_grad[0]
    keep = mine(grad, grad, d)[:, : FULL + 128]
    give = mine(grad, grad, 1 - d)[:, : FULL + 128]
    received = move(give, flip=1)
    grads = jnp.concatenate([keep, received], axis=0)

    local_x = inputs[0]
    pieces = gather_plane(local_x, norm_gain, received)
    scaled, slopes, ready, corr, inverse = forward(block, pieces, weights, grads)

    rows = jnp.pad(corr.reshape(2, TOK) / FEATS, ((0, 0), (0, 512 - TOK))).reshape(2, 2, BLK)
    extra = jnp.pad(rows, ((0, 0), (0, EXTRA - 2), (0, 0))).astype(BF)
    own_a, par_a, part_b, last_a, last_b = input_parts(order, slopes, weights, extra, ready)
    ring_y = move(last_a, dy=1, turn=True)
    up = move(last_b, dz=1, turn=True)
    theirs = weight_parts(other_core, scaled, after(ready, part_b))

    ring_y, up = after((ring_y, up), theirs)
    got = move(after(theirs, ring_y, up), dc=1)
    ring_y = add(own_a[1], ring_y).astype(BF)
    up, down = add(part_b[3], up).astype(BF), part_b[5]
    ring_y, up, down = after((ring_y, up, down))
    ours = weight_parts(this_core, scaled, after(ready, ring_y, up), got)
    parts = [ours[2 * k : 2 * k + 2] for k in range(NX)]
    ring_y = move(ring_y, dy=1, turn=True)
    up, down = move(up, dz=1, turn=True), move(down, dz=-1, turn=True)

    ring_y, up, down = after((ring_y, up, down), ours)
    ring_y = add(par_a[0], ring_y).astype(BF)
    up, down = add(part_b[2], up).astype(BF), add(part_b[6], down).astype(BF)
    ring_y, up, down = after((ring_y, up, down))
    x_next = move(parts[1], dx=1, turn=True)
    ring_y = move(ring_y, dy=1, turn=True)
    up, down = move(up, dz=1, turn=True), move(down, dz=-1, turn=True)

    line = add(own_a[0], ring_y).astype(BF)
    up, down = add(part_b[1], up).astype(BF), add(part_b[7], down).astype(BF)
    line, up, down, far_x, last_x = after((line, up, down, parts[2], parts[3]), x_next)
    up, down = move(up, dz=1, turn=True), move(down, dz=-1, turn=True)
    line = swap_z(line)
    x_across, x_back = move(far_x, dx=2), move(last_x, dx=-1, turn=True)

    column = add(part_b[0], up, down)
    sent = column.astype(BF)
    sum_b = add(column[0], *[move(sent[j], flip=j) for j in (1, 2, 3)])
    sum_a = jnp.sum(line.astype(F32), axis=0)
    x_across, x_back = after((x_across, x_back), sum_b)
    rows = add(parts[0], x_next, x_across, x_back)
    rows_0, rows_1 = rows[0], rows[1]
    keep = pick(rows_0, rows_1, d).astype(BF)
    got = move(pick(rows_1, rows_0, d).astype(BF), flip=1)

    def whole(start, shared):
        left, right = pick(keep, got, d), pick(got, keep, d)
        return jnp.concatenate(
            [
                left[:, start : start + FULL],
                left[:, shared : shared + HALF],
                right[:, shared : shared + HALF],
                right[:, start : start + FULL],
            ],
            axis=1,
        )

    gate_grad = whole(0, FULL)
    up_grad = whole(FULL + 128, FULL + HALF)

    normed_grad = jnp.concatenate([sum_a[EXTRA:], sum_b], axis=0)
    correction = sum_a[:2].reshape(512)[:TOK][:, None]
    inv = inverse[:TOK]
    x = local_x.astype(F32)
    input_grad = inv * (normed_grad * norm_gain) - x * inv * inv * inv * correction
    gain_part = jnp.sum(normed_grad * x * inv, axis=0).reshape(2, 128)
    gain_part = gain_part + move(gain_part, dc=1)
    gain_part = (
        gain_part + move(gain_part, dx=1) + move(gain_part, dx=-1) + move(gain_part, dx=2)
    )
    gain_grad = (gain_part + move(gain_part, flip=1)).reshape(BLK)
    return input_grad.astype(BF)[None], gain_grad, gate_grad, up_grad


def solution(mesh):
    placed = (
        P(("fsdp", "dp"), None, "tensor"),
        P("tensor"),
        P("fsdp", "tensor"),
        P("fsdp", "tensor"),
        P(("fsdp", "dp"), None, "tensor"),
    )
    return jax.shard_map(
        body,
        mesh=mesh,
        in_specs=placed,
        out_specs=(
            P(("fsdp", "dp"), None, "tensor"),
            P("tensor"),
            P(("fsdp", "dp"), "tensor"),
            P(("fsdp", "dp"), "tensor"),
        ),
        check_vma=False,
    )
```
